256 devices in a mesh: prow: 8 (over y, x_lo), pcol: 32 (over z, x_hi, core).
Axes of the slice: x: 4 (x_hi: 2, x_lo: 2; x = x_hi * 2 + x_lo), y: 4, z: 8, core: 2. Of those that a mesh axis runs over, the one named last changes fastest.
Arguments:
- pair: bfloat16 [768, 768, 128], P('prow', 'pcol'), may hold values from -6 to 6
- pair_mask: int32 [768, 768], P('prow', 'pcol'), may hold values 0 or 1
- in_gain: float32 [128], replicated, may hold values from 0.1 to 1.9
- in_bias: float32 [128], replicated, may hold values from -3 to 3
- input_proj: bfloat16 [128, 512], replicated, may hold values from -0.5 to 0.5
- gate_weight: bfloat16 [128, 128], replicated, may hold values from -0.5 to 0.5
- out_gain: float32 [128], replicated, may hold values from 0.1 to 1.9
- out_bias: float32 [128], replicated, may hold values from -3 to 3
- out_weight: bfloat16 [128, 128], replicated, may hold values from -0.5 to 0.5
Outputs:
- update: bfloat16 [768, 768, 128], P('prow', 'pcol')
The draws below stay inside these ranges and needn't reach their ends.
All inputs are finite; a program needn't handle non-finite values. No bound on the sum of `pair_mask` on one device may be relied on, other than what follows from the above.
Results may differ from the reference program's by a relative error of at most 0.0053.
Values may be sent and summed in bfloat16 or wider, within the bound.
No kernel may reach another device: no remote copies, remote signals or barrier semaphores. Data moves between devices by JAX's collectives and lax.ppermute only.
A program may use at most 128 MiB of HBM per device.

```python
import jax
import jax.numpy as jnp
from jax import lax

CH = 128
NTOK = 768


def set_ends(values, rng, smallest, largest):
    longest = values.shape.index(max(values.shape))
    spots = []
    for shift in (0, 1):
        where = [jax.random.randint(jax.random.fold_in(rng, axis), (), 0, length) for axis, length in enumerate(values.shape)]
        where[longest] = (where[longest] + shift) % values.shape[longest]
        spots.append(tuple(where))
    return values.at[spots[0]].set(smallest).at[spots[1]].set(largest)


def block_scale(own_key, dims, split, least, top_value):
    level = 1.0
    for axis_at, shards_of in split:
        steps = jax.random.uniform(jax.random.fold_in(jax.random.fold_in(own_key, 6), axis_at), (shards_of,), jnp.float32, least / len(split), top_value / len(split))
        level = level * jnp.repeat(jnp.exp(steps), dims[axis_at] // shards_of).reshape((-1,) + (1,) * (len(dims) - 1 - axis_at))
    return level


def normal_values(stream_key, shape, deviation, most, shards=(), dtype=jnp.bfloat16):
    factor_of = block_scale(stream_key, shape, shards, -0.22, 0.18) if shards else 1.0
    result = jax.random.normal(stream_key, shape, jnp.float32) * deviation * factor_of
    return jnp.minimum(jnp.maximum(result, -most), most).astype(dtype)


def setup_inputs(seed: int = 0) -> dict:
    keys = jax.random.split(jax.random.key(seed), 10)
    pair = normal_values(keys[0], (NTOK, NTOK, CH), 1.0, 6.0, ((0, 8), (1, 32)))
    pair_mask = set_ends((jax.random.randint(keys[1], (NTOK, NTOK), 0, 8) < 7).astype(jnp.int32), jax.random.fold_in(keys[1], 1), 0, 1)
    in_gain = jnp.clip(1.0 + 0.18 * jax.random.normal(keys[2], (CH,), jnp.float32), 0.1, 1.9)
    in_bias = normal_values(keys[3], (CH,), 0.5, 3.0, (), jnp.float32)
    input_proj = normal_values(keys[4], (CH, 4 * CH), CH ** -0.5, 0.5)
    gate_weight = normal_values(keys[5], (CH, CH), CH ** -0.5, 0.5)
    out_gain = jnp.clip(1.0 + 0.18 * jax.random.normal(keys[6], (CH,), jnp.float32), 0.1, 1.9)
    out_bias = normal_values(keys[7], (CH,), 0.5, 3.0, (), jnp.float32)
    out_weight = normal_values(keys[8], (CH, CH), CH ** -0.5, 0.5)
    return dict(pair=pair, pair_mask=pair_mask, in_gain=in_gain, in_bias=in_bias, input_proj=input_proj, gate_weight=gate_weight, out_gain=out_gain, out_bias=out_bias, out_weight=out_weight)


def layer_norm(values, gain, bias):
    mean = lax.optimization_barrier(jnp.mean(values, axis=-1, keepdims=True))
    centred = values - mean
    var = lax.optimization_barrier(jnp.mean(centred * centred, axis=-1, keepdims=True))
    return centred * jax.lax.rsqrt(var + 1e-05) * gain + bias

def reference(pair, pair_mask, in_gain, in_bias, input_proj, gate_weight, out_gain, out_bias, out_weight):
    normed_in = layer_norm(pair.astype(jnp.float32), in_gain, in_bias).astype(jnp.bfloat16)
    flat = normed_in.reshape(NTOK * NTOK, CH)
    proj = jnp.dot(flat, input_proj, preferred_element_type=jnp.float32).reshape(NTOK, NTOK, 4 * CH)
    live = pair_mask.astype(jnp.float32)[:, :, None]
    left = (live * jax.nn.sigmoid(proj[:, :, :CH]) * proj[:, :, CH:2 * CH]).astype(jnp.bfloat16)
    right = (live * jax.nn.sigmoid(proj[:, :, 2 * CH:3 * CH]) * proj[:, :, 3 * CH:]).astype(jnp.bfloat16)
    tri = jnp.einsum('ikc,jkc->ijc', left.astype(jnp.float32), right.astype(jnp.float32))
    normed_tri = layer_norm(tri, out_gain, out_bias).astype(jnp.bfloat16)
    gate = jax.nn.sigmoid(jnp.dot(flat, gate_weight, preferred_element_type=jnp.float32))
    mixed = jnp.dot(normed_tri.reshape(NTOK * NTOK, CH), out_weight, preferred_element_type=jnp.float32)
    return (gate * mixed).reshape(NTOK, NTOK, CH).astype(jnp.bfloat16)
```

```python
import jax
import jax.numpy as jnp
from jax import lax
from jax.sharding import Mesh
from jax.sharding import PartitionSpec as P

CHIPS = ("y", "xl", "z", "xh")


def layer_norm(values, gain, bias):
    mean = jnp.mean(values, axis=-1, keepdims=True)
    centred = values - mean
    var = jnp.mean(centred * centred, axis=-1, keepdims=True)
    return centred * lax.rsqrt(var + 1e-05) * gain + bias


def body(
    pair, pair_mask, in_gain, in_bias, input_proj, gate_weight, out_gain, out_bias, out_weight
):
    rows, cols, width = pair.shape
    normed_in = layer_norm(pair.astype(jnp.float32), in_gain, in_bias).astype(jnp.bfloat16)
    flat = normed_in.reshape(rows * cols, width)
    proj = jnp.dot(flat, input_proj, preferred_element_type=jnp.float32).reshape(
        rows, cols, 4 * width
    )
    live = pair_mask.astype(jnp.float32)[:, :, None]
    left = (live * jax.nn.sigmoid(proj[:, :, :width]) * proj[:, :, width : 2 * width]).astype(
        jnp.bfloat16
    )
    right = (
        live * jax.nn.sigmoid(proj[:, :, 2 * width : 3 * width]) * proj[:, :, 3 * width :]
    ).astype(jnp.bfloat16)
    both = jnp.stack([left, right]).transpose(3, 0, 2, 1)
    both = both.reshape(width, 2 * rows * cols // 128, 128)
    both = lax.all_to_all(both, CHIPS, 0, 0, tiled=True)
    both = both.reshape(8, 16, 2, cols, rows)
    left, right = both[:, :, 0], both[:, :, 1]
    part = jnp.einsum("pqki,rqkj->pirj", left, right, preferred_element_type=jnp.float32)
    part = part.reshape(8, rows, 16, 2, cols)
    core = lax.axis_index("core")
    mine = lax.dynamic_index_in_dim(part, core, 3, keepdims=False)
    other = lax.dynamic_index_in_dim(part, 1 - core, 3, keepdims=False)
    got = lax.ppermute(other, "core", [(0, 1), (1, 0)])
    tri = (mine + got).astype(jnp.bfloat16)
    tri = tri.transpose(0, 2, 1, 3).reshape(width, rows * cols // 128, 128)
    tri = lax.all_to_all(tri, CHIPS, 0, 0, tiled=True)
    tri = tri.reshape(width, rows * cols).T.astype(jnp.float32)
    normed_tri = layer_norm(tri, out_gain, out_bias).astype(jnp.bfloat16)
    gate = jax.nn.sigmoid(jnp.dot(flat, gate_weight, preferred_element_type=jnp.float32))
    mixed = jnp.dot(normed_tri, out_weight, preferred_element_type=jnp.float32)
    return (gate * mixed).reshape(rows, cols, width).astype(jnp.bfloat16)


def solution(mesh):
    fine = Mesh(mesh.devices.reshape(4, 2, 8, 2, 2), ("y", "xl", "z", "xh", "core"))
    split = P(("y", "xl"), ("z", "xh", "core"))
    return jax.shard_map(
        body,
        mesh=fine,
        in_specs=(split, split, P(), P(), P(), P(), P(), P(), P()),
        out_specs=split,
        check_vma=False,
    )
```

```python
import jax
import jax.numpy as jnp
from jax import lax
from jax.experimental import pallas as pl
from jax.experimental.pallas import tpu as pltpu
from jax.sharding import Mesh
from jax.sharding import PartitionSpec as P

CHIPS = ("y", "xl", "z", "xh")
LIMIT = 48 * 1024 * 1024
ROWS = 96
COLS = 24
CH = 128
SENT = 40
ORDER = ((0, 56, 16), (16, 24, 24), (40, 72, 24), (64, 0, 24), (88, 48, 8), (96, 0, 24), (120, 48, 8))
BF = jnp.bfloat16
F32 = jnp.float32


def dot(a, b, ca, cb):
    return lax.dot_general(a, b, (((ca,), (cb,)), ((), ())), preferred_element_type=F32)


def project_kernel(pair, mask, gain, bias, weight, sent, normed, rows, out):
    for at in range(0, ROWS * COLS, 256):
        x = pair[pl.ds(at, 256), :].astype(F32)
        mean = jnp.mean(x, axis=-1, keepdims=True)
        centred = x - mean
        var = jnp.mean(centred * centred, axis=-1, keepdims=True)
        x = (centred * lax.rsqrt(var + 1e-05) * gain[...] + bias[...]).astype(BF)
        normed[pl.ds(at, 256), :] = x
        rows[pl.ds(at, 256), :] = x.astype(F32)

    lane = lax.broadcasted_iota(jnp.int32, (ROWS, CH), 1)
    token = lax.broadcasted_iota(jnp.int32, (ROWS, CH), 0)
    source = lane
    for start, first, count in ORDER:
        source = jnp.where((lane >= start) & (lane < start + count), lane - start + first, source)
    spread = (source == token).astype(F32).astype(BF)
    live = dot(mask[...].astype(F32).astype(BF), spread, 1, 0)

    turned = weight[...].astype(F32).T.astype(BF)
    at_lane = lax.broadcasted_iota(jnp.int32, (CH, CH), 1)

    def column(k):
        x = rows[pl.ds(k, ROWS, stride=COLS), :]
        x = jnp.concatenate([x[first : first + count] for _, first, count in ORDER], axis=0)
        x = x.astype(BF)
        proj = dot(turned, x, 1, 1)
        m = live[k : k + 1, :]
        left = m * jax.nn.sigmoid(proj[:CH]) * proj[CH : 2 * CH]
        right = m * jax.nn.sigmoid(proj[2 * CH : 3 * CH]) * proj[3 * CH :]
        out[pl.ds(k, CH, stride=SENT), :] = jnp.where(at_lane < ROWS, left, right)
        return right

    for k in range(8):
        low = column(k)
        high = column(k + 8)
        out[pl.ds(24 + k, CH, stride=SENT), :] = jnp.where(
            at_lane < 64, low, pltpu.roll(high, 64, 1)
        )
        out[pl.ds(32 + k, CH, stride=SENT), :] = column(k + 16)
    sent[...] = out[...].reshape(CH, SENT, CH).astype(BF)


def product_kernel(core, own, other, sent):
    shift = jnp.where(core[0] == 0, 32, 112)
    lane = lax.broadcasted_iota(jnp.int32, (384, CH), 1)
    lefts, rights = [], []
    for block in range(8):
        ls, rs = [], []
        for ref in (own, other):
            v = ref[pl.ds(block * 16, 16)].astype(F32)
            left = v[:, :24].reshape(384, CH)
            mid = v[:, 24:32]
            right = jnp.concatenate(
                [mid, pltpu.roll(mid, 64, 2), v[:, 32:40]], axis=1
            ).reshape(384, CH)
            right = jnp.where(lane < 64, right, left)
            rs.append(pltpu.roll(right, shift, 1))
            ls.append(left.astype(BF))
        lefts.append(jnp.concatenate(ls, axis=0))
        rights.append(jnp.concatenate(rs, axis=0))
    lane = lax.broadcasted_iota(jnp.int32, (768, CH), 1)
    left = jnp.concatenate(lefts, axis=1)
    for pair in range(4):
        right = jnp.where(lane < 64, rights[2 * pair], pltpu.roll(rights[2 * pair + 1], 64, 1))
        tri = dot(right.astype(BF).T, left, 1, 0).astype(BF)
        for part, at in enumerate((0, 24, 64, 88)):
            for block in range(8):
                sent[block * 16 + pair * 4 + part] = tri[
                    at : at + 24, block * CH : (block + 1) * CH
                ]


def finish_kernel(tri, gate, gain, bias, weight, update, cols, out):
    cols[...] = tri[...].astype(F32).reshape(CH * COLS, CH)
    for j in range(COLS):
        v = cols[pl.ds(j, CH, stride=COLS), :]
        mean = jnp.mean(v, axis=0, keepdims=True)
        centred = v - mean
        var = jnp.mean(centred * centred, axis=0, keepdims=True)
        v = (centred * lax.rsqrt(var + 1e-05) * gain[...] + bias[...]).astype(BF)
        mixed = dot(v, weight[...], 0, 0)
        place = {first: mixed[start : start + count] for start, first, count in ORDER[:5]}
        out[pl.ds(j, ROWS, stride=COLS), :] = jnp.concatenate(
            [place[first] for first in sorted(place)], axis=0
        )
    for at in range(0, ROWS * COLS, 256):
        here = pl.ds(at, 256)
        update[here, :] = (gate[here, :] * out[here, :]).astype(BF)


VMEM = pl.BlockSpec(memory_space=pltpu.VMEM)
SMEM = pl.BlockSpec(memory_space=pltpu.SMEM)
PARAMS = pltpu.CompilerParams(vmem_limit_bytes=LIMIT)


def body(
    pair, pair_mask, in_gain, in_bias, input_proj, gate_weight, out_gain, out_bias, out_weight
):
    tokens = ROWS * COLS
    sent, normed = pl.pallas_call(
        project_kernel,
        out_shape=(
            jax.ShapeDtypeStruct((CH, SENT, CH), BF),
            jax.ShapeDtypeStruct((tokens, CH), BF),
        ),
        in_specs=[VMEM] * 5,
        out_specs=(VMEM, VMEM),
        scratch_shapes=[pltpu.VMEM((tokens, CH), F32), pltpu.VMEM((CH * SENT, CH), F32)],
        compiler_params=PARAMS,
        name="project",
    )(
        pair.reshape(tokens, CH),
        pair_mask.T,
        in_gain.reshape(1, CH),
        in_bias.reshape(1, CH),
        input_proj,
    )
    own = lax.all_to_all(sent, CHIPS, 0, 0, tiled=True)
    other = lax.ppermute(own, "core", [(0, 1), (1, 0)])
    gate = jax.nn.sigmoid(jnp.dot(normed, gate_weight, preferred_element_type=F32))
    core = lax.axis_index("core").astype(jnp.int32).reshape(1)
    tri = pl.pallas_call(
        product_kernel,
        out_shape=jax.ShapeDtypeStruct((CH, COLS, CH), BF),
        in_specs=[SMEM, VMEM, VMEM],
        out_specs=VMEM,
        compiler_params=PARAMS,
        name="product",
    )(core, own, other)
    tri = lax.all_to_all(tri, CHIPS, 0, 0, tiled=True)
    update = pl.pallas_call(
        finish_kernel,
        out_shape=jax.ShapeDtypeStruct((tokens, CH), BF),
        in_specs=[VMEM] * 5,
        out_specs=VMEM,
        scratch_shapes=[pltpu.VMEM((CH * COLS, CH), F32), pltpu.VMEM((tokens, CH), F32)],
        compiler_params=PARAMS,
        name="finish",
    )(tri, gate, out_gain.reshape(CH, 1), out_bias.reshape(CH, 1), out_weight)
    return update.reshape(ROWS, COLS, CH)


def solution(mesh):
    fine = Mesh(mesh.devices.reshape(4, 2, 8, 2, 2), ("y", "xl", "z", "xh", "core"))
    split = P(("y", "xl"), ("z", "xh", "core"))
    return jax.shard_map(
        body,
        mesh=fine,
        in_specs=(split, split, P(), P(), P(), P(), P(), P(), P()),
        out_specs=split,
        check_vma=False,
    )
```

```python
import jax
import jax.numpy as jnp
from jax import lax
from jax.experimental import pallas as pl
from jax.experimental.pallas import tpu as pltpu
from jax.sharding import Mesh
from jax.sharding import PartitionSpec as P

CHIPS = ("y", "xl", "z", "xh")
LIMIT = 48 * 1024 * 1024
ROWS = 96
COLS = 24
CH = 128
SENT = 36
BACK = 18
TOKENS = ROWS * COLS
ORDER = ((0, 56, 16), (16, 24, 24), (40, 72, 24), (64, 0, 24), (88, 48, 8), (96, 0, 24), (120, 48, 8))
BF = jnp.bfloat16
F32 = jnp.float32


def dot(a, b, ca, cb):
    return lax.dot_general(a, b, (((ca,), (cb,)), ((), ())), preferred_element_type=F32)


def project_kernel(
    pair, mask, gain, bias, weight, sent, normed, pair_v, mask_v, gain_v, bias_v, weight_v, rows, out, sems
):
    parts = 4
    step = TOKENS // parts
    here = [pl.ds(part * step, step) for part in range(parts)]
    copies = [
        pltpu.make_async_copy(a, b, sems.at[n])
        for n, (a, b) in enumerate(
            [(gain, gain_v), (bias, bias_v)]
            + [(pair.at[h, :], pair_v.at[h, :]) for h in here]
            + [(mask, mask_v), (weight, weight_v)]
        )
    ]
    for copy in copies:
        copy.start()
    copies[0].wait()
    copies[1].wait()
    for part in range(parts):
        copies[2 + part].wait()
        for at in range(part * step, (part + 1) * step, 192):
            x = pair_v[pl.ds(at, 192), :].astype(F32)
            mean = jnp.mean(x, axis=-1, keepdims=True)
            centred = x - mean
            var = jnp.mean(centred * centred, axis=-1, keepdims=True)
            x = (centred * lax.rsqrt(var + 1e-05) * gain_v[...] + bias_v[...]).astype(BF)
            normed[pl.ds(at, 192), :] = x
            rows[pl.ds(at, 192), :] = x.astype(F32)
    copies[-2].wait()
    copies[-1].wait()

    lane = lax.broadcasted_iota(jnp.int32, (ROWS, CH), 1)
    token = lax.broadcasted_iota(jnp.int32, (ROWS, CH), 0)
    source = lane
    for start, first, count in ORDER:
        source = jnp.where((lane >= start) & (lane < start + count), lane - start + first, source)
    spread = (source == token).astype(F32).astype(BF)
    live = dot(mask_v[...].astype(F32).astype(BF), spread, 1, 0)

    turned = weight_v[...].astype(F32).T.astype(BF)
    at_lane = lax.broadcasted_iota(jnp.int32, (CH, CH), 1)

    def column(k):
        x = rows[pl.ds(k, ROWS, stride=COLS), :]
        x = jnp.concatenate([x[first : first + count] for _, first, count in ORDER], axis=0)
        x = x.astype(BF)
        proj = dot(turned, x, 1, 1)
        m = live[k : k + 1, :]
        left = m * jax.nn.sigmoid(proj[:CH]) * proj[CH : 2 * CH]
        right = m * jax.nn.sigmoid(proj[2 * CH : 3 * CH]) * proj[3 * CH :]
        out[pl.ds(k, CH, stride=SENT), :] = jnp.where(at_lane < ROWS, left, right)
        return right

    for k in range(12):
        low = column(k)
        high = column(k + 12)
        out[pl.ds(24 + k, CH, stride=SENT), :] = jnp.where(
            at_lane < 64, low, pltpu.roll(high, 64, 1)
        )
    sent[...] = out[...].astype(BF)


def operands(chunks, wide, shift):
    wide[...] = chunks[...].astype(F32)
    lane = lax.broadcasted_iota(jnp.int32, (384, CH), 1)
    lefts, rights = [], []
    for block in range(8):
        at = block * 16 * SENT
        left = jnp.concatenate(
            [wide[pl.ds(at + k, 16, stride=SENT), :] for k in range(24)], axis=0
        )
        mid = jnp.concatenate(
            [wide[pl.ds(at + 24 + k, 16, stride=SENT), :] for k in range(12)], axis=0
        )
        right = jnp.concatenate([mid, pltpu.roll(mid, 64, 1)], axis=0)
        right = jnp.where(lane < 64, right, left)
        rights.append(pltpu.roll(right, shift, 1))
        lefts.append(left.astype(BF))
    pairs = [
        jnp.where(lane < 64, rights[2 * n], pltpu.roll(rights[2 * n + 1], 64, 1)).astype(BF)
        for n in range(4)
    ]
    return jnp.concatenate(lefts, axis=1), pairs


def product_own_kernel(core, chunks, total, wide):
    left, rights = operands(chunks, wide, jnp.where(core[0] == 0, 32, 112))
    for n in range(4):
        total[pl.ds(n * CH, CH), :] = dot(rights[n].T, left, 1, 0)


def product_other_kernel(core, chunks, total, sent, wide, packed):
    left, rights = operands(chunks, wide, jnp.where(core[0] == 0, 32, 112))
    lane = lax.broadcasted_iota(jnp.int32, (BACK, CH), 1)
    for n in range(4):
        tri = total[pl.ds(n * CH, CH), :] + dot(rights[n].T, left, 1, 0)
        for part, at in enumerate((0, 24, 64, 88)):
            for block in range(8):
                here = tri[at : at + 24, block * CH : (block + 1) * CH]
                tail = here[BACK:]
                tail = jnp.concatenate([pltpu.roll(tail, 96 - 32 * g, 1) for g in range(3)], axis=0)
                packed[pl.ds((block * 16 + n * 4 + part) * BACK, BACK), :] = jnp.where(
                    lane < ROWS, here[:BACK], tail
                )
    sent[...] = packed[...].astype(BF)


def finish_kernel(tri, gate, gain, bias, weight, update, cols, out, done, sems):
    cols[...] = tri[...].astype(F32)
    for row in range(BACK):
        v = cols[pl.ds(row, CH, stride=BACK), :]
        mean = jnp.mean(v, axis=0, keepdims=True)
        centred = v - mean
        var = jnp.mean(centred * centred, axis=0, keepdims=True)
        v = (centred * lax.rsqrt(var + 1e-05) * gain[...] + bias[...]).astype(BF)
        mixed = dot(v, weight[...], 0, 0)
        for start, first, count in ORDER[:5]:
            out[pl.ds(first * COLS + row, count, stride=COLS), :] = mixed[start : start + count]
        group = row // 6
        for start, first, count in ORDER[:5]:
            low, high = max(start, 32 * group), min(start + count, 32 * group + 32)
            if low < high:
                out[pl.ds((first + low - start) * COLS + BACK + row % 6, high - low, stride=COLS), :] = (
                    mixed[ROWS + low - 32 * group : ROWS + high - 32 * group]
                )
    parts = 4
    step = TOKENS // parts
    copies = []
    for part in range(parts):
        here = pl.ds(part * step, step)
        done[here, :] = (gate[here, :] * out[here, :]).astype(BF)
        copies.append(pltpu.make_async_copy(done.at[here, :], update.at[here, :], sems.at[part]))
        copies[-1].start()
    for copy in copies:
        copy.wait()


VMEM = pl.BlockSpec(memory_space=pltpu.VMEM)
SMEM = pl.BlockSpec(memory_space=pltpu.SMEM)
HBM = pl.BlockSpec(memory_space=pltpu.HBM)
PARAMS = pltpu.CompilerParams(vmem_limit_bytes=LIMIT)


def body(
    pair, pair_mask, in_gain, in_bias, input_proj, gate_weight, out_gain, out_bias, out_weight
):
    sent, normed = pl.pallas_call(
        project_kernel,
        out_shape=(
            jax.ShapeDtypeStruct((CH * SENT, CH), BF),
            jax.ShapeDtypeStruct((TOKENS, CH), BF),
        ),
        in_specs=[HBM] * 5,
        out_specs=(VMEM, VMEM),
        scratch_shapes=[
            pltpu.VMEM((TOKENS, CH), BF),
            pltpu.VMEM((COLS, ROWS), jnp.int32),
            pltpu.VMEM((1, CH), F32),
            pltpu.VMEM((1, CH), F32),
            pltpu.VMEM((CH, 4 * CH), BF),
            pltpu.VMEM((TOKENS, CH), F32),
            pltpu.VMEM((CH * SENT, CH), F32),
            pltpu.SemaphoreType.DMA((8,)),
        ],
        compiler_params=pltpu.CompilerParams(vmem_limit_bytes=56 * 1024 * 1024),
        name="project",
    )(
        pair.reshape(TOKENS, CH),
        pair_mask.T,
        in_gain.reshape(1, CH),
        in_bias.reshape(1, CH),
        input_proj,
    )
    own = lax.all_to_all(sent.reshape(CH, 9, 4, CH), CHIPS, 0, 0, tiled=True)
    other = lax.ppermute(own, "core", [(0, 1), (1, 0)])
    gate = jax.nn.sigmoid(jnp.dot(normed, gate_weight, preferred_element_type=F32))
    core = lax.axis_index("core").astype(jnp.int32).reshape(1)
    total = pl.pallas_call(
        product_own_kernel,
        out_shape=jax.ShapeDtypeStruct((4 * CH, 8 * CH), F32),
        in_specs=[SMEM, VMEM],
        out_specs=VMEM,
        scratch_shapes=[pltpu.VMEM((CH * SENT, CH), F32)],
        compiler_params=PARAMS,
        cost_estimate=pl.CostEstimate(flops=4 * 10**8, bytes_accessed=4 * 10**6, transcendentals=0),
        name="product_own",
    )(core, own.reshape(CH * SENT, CH))
    tri = pl.pallas_call(
        product_other_kernel,
        out_shape=jax.ShapeDtypeStruct((CH * BACK, CH), BF),
        in_specs=[SMEM, VMEM, VMEM],
        out_specs=VMEM,
        scratch_shapes=[pltpu.VMEM((CH * SENT, CH), F32), pltpu.VMEM((CH * BACK, CH), F32)],
        compiler_params=PARAMS,
        name="product_other",
    )(core, other.reshape(CH * SENT, CH), total)
    tri = lax.all_to_all(tri.reshape(CH, 9, 2, CH), CHIPS, 0, 0, tiled=True)
    update = pl.pallas_call(
        finish_kernel,
        out_shape=jax.ShapeDtypeStruct((TOKENS, CH), BF),
        in_specs=[VMEM] * 5,
        out_specs=HBM,
        scratch_shapes=[
            pltpu.VMEM((CH * BACK, CH), F32),
            pltpu.VMEM((TOKENS, CH), F32),
            pltpu.VMEM((TOKENS, CH), BF),
            pltpu.SemaphoreType.DMA((4,)),
        ],
        compiler_params=PARAMS,
        name="finish",
    )(tri.reshape(CH * BACK, CH), gate, out_gain.reshape(CH, 1), out_bias.reshape(CH, 1), out_weight)
    return update.reshape(ROWS, COLS, CH)


def solution(mesh):
    fine = Mesh(mesh.devices.reshape(4, 2, 8, 2, 2), ("y", "xl", "z", "xh", "core"))
    split = P(("y", "xl"), ("z", "xh", "core"))
    return jax.shard_map(
        body,
        mesh=fine,
        in_specs=(split, split, P(), P(), P(), P(), P(), P(), P()),
        out_specs=split,
        check_vma=False,
    )
```

```python
import jax
import jax.numpy as jnp
from jax import lax
from jax.experimental import pallas as pl
from jax.experimental.pallas import tpu as pltpu
from jax.sharding import Mesh
from jax.sharding import PartitionSpec as P

CHIPS = ("y", "xl", "z", "xh")
LIMIT = 48 * 1024 * 1024
ROWS = 96
COLS = 24
CH = 128
SENT = 36
BACK = 18
TOKENS = ROWS * COLS
ORDER = ((0, 56, 16), (16, 24, 24), (40, 72, 24), (64, 0, 24), (88, 48, 8), (96, 0, 24), (120, 48, 8))
BF = jnp.bfloat16
F32 = jnp.float32


def dot(a, b, ca, cb):
    return lax.dot_general(a, b, (((ca,), (cb,)), ((), ())), preferred_element_type=F32)


def sigmoid(v):
    return 0.5 * jnp.tanh(0.5 * v) + 0.5


def project_kernel(
    pair, mask, gain, bias, weight, sent, normed, pair_v, mask_v, gain_v, bias_v, weight_v, rows, out, sems
):
    parts = 4
    step = TOKENS // parts
    here = [pl.ds(part * step, step) for part in range(parts)]
    copies = [
        pltpu.make_async_copy(a, b, sems.at[n])
        for n, (a, b) in enumerate(
            [(gain, gain_v), (bias, bias_v)]
            + [(pair.at[h, :], pair_v.at[h, :]) for h in here]
            + [(mask, mask_v), (weight, weight_v)]
        )
    ]
    for copy in copies:
        copy.start()
    copies[0].wait()
    copies[1].wait()
    for part in range(parts):
        copies[2 + part].wait()
        for at in range(part * step, (part + 1) * step, 192):
            x = pair_v[pl.ds(at, 192), :].astype(F32)
            mean = jnp.mean(x, axis=-1, keepdims=True)
            centred = x - mean
            var = jnp.mean(centred * centred, axis=-1, keepdims=True)
            x = (centred * lax.rsqrt(var + 1e-05) * gain_v[...] + bias_v[...]).astype(BF)
            normed[pl.ds(at, 192), :] = x
            rows[pl.ds(at, 192), :] = x.astype(F32)
    copies[-2].wait()
    copies[-1].wait()

    lane = lax.broadcasted_iota(jnp.int32, (ROWS, CH), 1)
    token = lax.broadcasted_iota(jnp.int32, (ROWS, CH), 0)
    source = lane
    for start, first, count in ORDER:
        source = jnp.where((lane >= start) & (lane < start + count), lane - start + first, source)
    spread = (source == token).astype(F32).astype(BF)
    live = dot(mask_v[...].astype(F32).astype(BF), spread, 1, 0)

    turned = weight_v[...].astype(F32).T.astype(BF)
    at_lane = lax.broadcasted_iota(jnp.int32, (CH, CH), 1)

    def column(k):
        x = rows[pl.ds(k, ROWS, stride=COLS), :]
        x = jnp.concatenate([x[first : first + count] for _, first, count in ORDER], axis=0)
        x = x.astype(BF)
        proj = dot(turned, x, 1, 1)
        m = live[k : k + 1, :]
        left = m * sigmoid(proj[:CH]) * proj[CH : 2 * CH]
        right = m * sigmoid(proj[2 * CH : 3 * CH]) * proj[3 * CH :]
        out[pl.ds(k, CH, stride=SENT), :] = jnp.where(at_lane < ROWS, left, right)
        return right

    for k in range(12):
        low = column(k)
        high = column(k + 12)
        out[pl.ds(24 + k, CH, stride=SENT), :] = jnp.where(
            at_lane < 64, low, pltpu.roll(high, 64, 1)
        )
    sent[...] = out[...].astype(BF)


def operands(chunks, wide, shift):
    wide[...] = chunks[...].astype(F32)
    lane = lax.broadcasted_iota(jnp.int32, (384, CH), 1)
    lefts, rights = [], []
    for block in range(8):
        at = block * 16 * SENT
        left = jnp.concatenate(
            [wide[pl.ds(at + k, 16, stride=SENT), :] for k in range(24)], axis=0
        )
        mid = jnp.concatenate(
            [wide[pl.ds(at + 24 + k, 16, stride=SENT), :] for k in range(12)], axis=0
        )
        right = jnp.concatenate([mid, pltpu.roll(mid, 64, 1)], axis=0)
        right = jnp.where(lane < 64, right, left)
        rights.append(pltpu.roll(right, shift, 1))
        lefts.append(left.astype(BF))
    pairs = [
        jnp.where(lane < 64, rights[2 * n], pltpu.roll(rights[2 * n + 1], 64, 1)).astype(BF)
        for n in range(4)
    ]
    return jnp.concatenate(lefts, axis=1), pairs


def product_own_kernel(
    core, chunks, normed, gate_weight, gain, bias, weight, total, gate, gains, biases, weights, wide
):
    left, rights = operands(chunks, wide, jnp.where(core[0] == 0, 32, 112))
    for n in range(4):
        total[pl.ds(n * CH, CH), :] = dot(rights[n].T, left, 1, 0)
    for at in range(0, TOKENS, 256):
        here = pl.ds(at, 256)
        gate[here, :] = sigmoid(dot(normed[here, :], gate_weight[...], 1, 0))
    gains[...] = jnp.broadcast_to(gain[...], (CH, CH)).T
    biases[...] = jnp.broadcast_to(bias[...], (CH, CH)).T
    weights[...] = weight[...]


def product_other_kernel(core, chunks, total, sent, wide, packed):
    left, rights = operands(chunks, wide, jnp.where(core[0] == 0, 32, 112))
    lane = lax.broadcasted_iota(jnp.int32, (BACK, CH), 1)
    for n in range(4):
        tri = total[pl.ds(n * CH, CH), :] + dot(rights[n].T, left, 1, 0)
        for part, at in enumerate((0, 24, 64, 88)):
            for block in range(8):
                here = tri[at : at + 24, block * CH : (block + 1) * CH]
                tail = here[BACK:]
                tail = jnp.concatenate([pltpu.roll(tail, 96 - 32 * g, 1) for g in range(3)], axis=0)
                packed[pl.ds((block * 16 + n * 4 + part) * BACK, BACK), :] = jnp.where(
                    lane < ROWS, here[:BACK], tail
                )
    sent[...] = packed[...].astype(BF)


def finish_kernel(tri, gate, gain, bias, weight, update, cols, out, done, sems):
    cols[...] = tri[...].astype(F32)
    for row in range(BACK):
        v = cols[pl.ds(row, CH, stride=BACK), :]
        mean = jnp.mean(v, axis=0, keepdims=True)
        centred = v - mean
        var = jnp.mean(centred * centred, axis=0, keepdims=True)
        v = (centred * lax.rsqrt(var + 1e-05) * gain[...] + bias[...]).astype(BF)
        mixed = dot(v, weight[...], 0, 0)
        for start, first, count in ORDER[:5]:
            out[pl.ds(first * COLS + row, count, stride=COLS), :] = mixed[start : start + count]
        group = row // 6
        for start, first, count in ORDER[:5]:
            low, high = max(start, 32 * group), min(start + count, 32 * group + 32)
            if low < high:
                out[pl.ds((first + low - start) * COLS + BACK + row % 6, high - low, stride=COLS), :] = (
                    mixed[ROWS + low - 32 * group : ROWS + high - 32 * group]
                )
    parts = 4
    step = TOKENS // parts
    copies = []
    for part in range(parts):
        here = pl.ds(part * step, step)
        done[here, :] = (gate[here, :] * out[here, :]).astype(BF)
        copies.append(pltpu.make_async_copy(done.at[here, :], update.at[here, :], sems.at[part]))
        copies[-1].start()
    for copy in copies:
        copy.wait()


VMEM = pl.BlockSpec(memory_space=pltpu.VMEM)
SMEM = pl.BlockSpec(memory_space=pltpu.SMEM)
HBM = pl.BlockSpec(memory_space=pltpu.HBM)
PARAMS = pltpu.CompilerParams(vmem_limit_bytes=LIMIT)


def in_hbm(x):
    return pltpu.with_memory_space_constraint(x, pltpu.HBM)


def body(
    pair, pair_mask, in_gain, in_bias, input_proj, gate_weight, out_gain, out_bias, out_weight
):
    sent, normed = pl.pallas_call(
        project_kernel,
        out_shape=(
            pltpu.VMEM((CH * SENT, CH), BF),
            pltpu.VMEM((TOKENS, CH), BF),
        ),
        in_specs=[HBM] * 5,
        out_specs=(VMEM, VMEM),
        scratch_shapes=[
            pltpu.VMEM((TOKENS, CH), BF),
            pltpu.VMEM((COLS, ROWS), jnp.int32),
            pltpu.VMEM((1, CH), F32),
            pltpu.VMEM((1, CH), F32),
            pltpu.VMEM((CH, 4 * CH), BF),
            pltpu.VMEM((TOKENS, CH), F32),
            pltpu.VMEM((CH * SENT, CH), F32),
            pltpu.SemaphoreType.DMA((8,)),
        ],
        compiler_params=PARAMS,
        name="project",
    )(
        in_hbm(pair.reshape(TOKENS, CH)),
        in_hbm(pair_mask.T),
        in_hbm(in_gain.reshape(1, CH)),
        in_hbm(in_bias.reshape(1, CH)),
        in_hbm(input_proj),
    )
    own = lax.all_to_all(sent.reshape(CH, 9, 4, CH), CHIPS, 0, 0, tiled=True)
    other = lax.ppermute(own, "core", [(0, 1), (1, 0)])
    core = lax.axis_index("core").astype(jnp.int32).reshape(1)
    total, gate, gains, biases, weights = pl.pallas_call(
        product_own_kernel,
        out_shape=(
            pltpu.VMEM((4 * CH, 8 * CH), F32),
            pltpu.VMEM((TOKENS, CH), F32),
            pltpu.VMEM((CH, CH), F32),
            pltpu.VMEM((CH, CH), F32),
            pltpu.VMEM((CH, CH), BF),
        ),
        in_specs=[SMEM] + [VMEM] * 6,
        out_specs=[VMEM] * 5,
        scratch_shapes=[pltpu.VMEM((CH * SENT, CH), F32)],
        compiler_params=PARAMS,
        cost_estimate=pl.CostEstimate(flops=4 * 10**8, bytes_accessed=4 * 10**6, transcendentals=0),
        name="product_own",
    )(
        core,
        own.reshape(CH * SENT, CH),
        normed,
        gate_weight,
        out_gain.reshape(1, CH),
        out_bias.reshape(1, CH),
        out_weight,
    )
    tri = pl.pallas_call(
        product_other_kernel,
        out_shape=pltpu.VMEM((CH * BACK, CH), BF),
        in_specs=[SMEM, VMEM, VMEM],
        out_specs=VMEM,
        scratch_shapes=[pltpu.VMEM((CH * SENT, CH), F32), pltpu.VMEM((CH * BACK, CH), F32)],
        compiler_params=PARAMS,
        name="product_other",
    )(core, other.reshape(CH * SENT, CH), total)
    tri = lax.all_to_all(tri.reshape(CH, 9, 2, CH), CHIPS, 0, 0, tiled=True)
    update = pl.pallas_call(
        finish_kernel,
        out_shape=jax.ShapeDtypeStruct((TOKENS, CH), BF),
        in_specs=[VMEM] * 5,
        out_specs=HBM,
        scratch_shapes=[
            pltpu.VMEM((CH * BACK, CH), F32),
            pltpu.VMEM((TOKENS, CH), F32),
            pltpu.VMEM((TOKENS, CH), BF),
            pltpu.SemaphoreType.DMA((4,)),
        ],
        compiler_params=PARAMS,
        name="finish",
    )(tri.reshape(CH * BACK, CH), gate, gains, biases, weights)
    return update.reshape(ROWS, COLS, CH)


def solution(mesh):
    fine = Mesh(mesh.devices.reshape(4, 2, 8, 2, 2), ("y", "xl", "z", "xh", "core"))
    split = P(("y", "xl"), ("z", "xh", "core"))
    return jax.shard_map(
        body,
        mesh=fine,
        in_specs=(split, split, P(), P(), P(), P(), P(), P(), P()),
        out_specs=split,
        check_vma=False,
    )
```

```python
import jax
import jax.numpy as jnp
from jax import lax
from jax.experimental import pallas as pl
from jax.experimental.pallas import tpu as pltpu
from jax.sharding import Mesh
from jax.sharding import PartitionSpec as P

CHIPS = ("xl", "y", "z", "xh")
LIMIT = 48 * 1024 * 1024
ROWS = 96
COLS = 24
CH = 128
SENT = 36
BACK = 18
TOKENS = ROWS * COLS
ORDER = ((0, 56, 16), (16, 24, 24), (40, 72, 24), (64, 0, 24), (88, 48, 8), (96, 0, 24), (120, 48, 8))
BF = jnp.bfloat16
F32 = jnp.float32


def dot(a, b, ca, cb):
    return lax.dot_general(a, b, (((ca,), (cb,)), ((), ())), preferred_element_type=F32)


def sigmoid(v):
    return 0.5 * jnp.tanh(0.5 * v) + 0.5


def project_kernel(
    pair, mask, gain, bias, weight, sent, normed, pair_v, mask_v, gain_v, bias_v, weight_v, rows, out, sems
):
    parts = 1
    step = TOKENS // parts
    here = [pl.ds(part * step, step) for part in range(parts)]
    copies = [
        pltpu.make_async_copy(a, b, sems.at[n])
        for n, (a, b) in enumerate(
            [(mask, mask_v), (weight, weight_v), (gain, gain_v), (bias, bias_v)]
            + [(pair.at[h, :], pair_v.at[h, :]) for h in here]
        )
    ]
    for copy in copies:
        copy.start()
    lane = lax.broadcasted_iota(jnp.int32, (ROWS, CH), 1)
    token = lax.broadcasted_iota(jnp.int32, (ROWS, CH), 0)
    source = lane
    for start, first, count in ORDER:
        source = jnp.where((lane >= start) & (lane < start + count), lane - start + first, source)
    spread = (source == token).astype(F32).astype(BF)
    copies[0].wait()
    copies[1].wait()
    live = dot(mask_v[...].astype(F32).astype(BF), spread, 1, 0)
    turned = weight_v[...].astype(F32).T.astype(BF)
    at_lane = lax.broadcasted_iota(jnp.int32, (CH, CH), 1)

    copies[2].wait()
    copies[3].wait()
    for part in range(parts):
        copies[4 + part].wait()
        for at in range(part * step, (part + 1) * step, 192):
            x = pair_v[pl.ds(at, 192), :].astype(F32)
            mean = jnp.mean(x, axis=-1, keepdims=True)
            centred = x - mean
            var = jnp.mean(centred * centred, axis=-1, keepdims=True)
            x = (centred * lax.rsqrt(var + 1e-05) * gain_v[...] + bias_v[...]).astype(BF)
            normed[pl.ds(at, 192), :] = x
            rows[pl.ds(at, 192), :] = x.astype(F32)

    def column(k):
        x = rows[pl.ds(k, ROWS, stride=COLS), :]
        x = jnp.concatenate([x[first : first + count] for _, first, count in ORDER], axis=0)
        x = x.astype(BF)
        proj = dot(turned, x, 1, 1)
        m = live[k : k + 1, :]
        left = m * sigmoid(proj[:CH]) * proj[CH : 2 * CH]
        right = m * sigmoid(proj[2 * CH : 3 * CH]) * proj[3 * CH :]
        out[pl.ds(k, CH, stride=SENT), :] = jnp.where(at_lane < ROWS, left, right)
        return right

    for k in range(12):
        low = column(k)
        high = column(k + 12)
        out[pl.ds(24 + k, CH, stride=SENT), :] = jnp.where(
            at_lane < 64, low, pltpu.roll(high, 64, 1)
        )
    sent[...] = out[...].astype(BF)


SIZES = {"y": 4, "xl": 2, "z": 8, "xh": 2}
STEP, span = {}, 1
for axis in reversed(CHIPS):
    STEP[axis], span = span, span * SIZES[axis]


def rank_of(block, z, xh):
    return block // 2 * STEP["y"] + block % 2 * STEP["xl"] + z * STEP["z"] + xh * STEP["xh"]


def operands(chunks, wide, shift):
    wide[...] = chunks[...].astype(F32)
    lane = lax.broadcasted_iota(jnp.int32, (384, CH), 1)
    lefts, rights = [], []
    for block in range(8):
        starts = [rank_of(block, 0, xh) * SENT for xh in range(2)]

        def gather(ks):
            return jnp.concatenate(
                [wide[pl.ds(at + k, 8, stride=SENT * STEP["z"]), :] for k in ks for at in starts],
                axis=0,
            )

        left = gather(range(24))
        mid = gather(range(24, SENT))
        right = jnp.concatenate([mid, pltpu.roll(mid, 64, 1)], axis=0)
        right = jnp.where(lane < 64, right, left)
        rights.append(pltpu.roll(right, shift, 1))
        lefts.append(left.astype(BF))
    pairs = [
        jnp.where(lane < 64, rights[2 * n], pltpu.roll(rights[2 * n + 1], 64, 1)).astype(BF)
        for n in range(4)
    ]
    return jnp.concatenate(lefts, axis=1), pairs


def product_own_kernel(
    core, chunks, normed, gate_weight, gain, bias, weight, total, gate, gains, biases, weights, wide
):
    left, rights = operands(chunks, wide, jnp.where(core[0] == 0, 32, 112))
    for n in range(4):
        total[pl.ds(n * CH, CH), :] = dot(rights[n].T, left, 1, 0)
    for at in range(0, TOKENS, 256):
        here = pl.ds(at, 256)
        gate[here, :] = sigmoid(dot(normed[here, :], gate_weight[...], 1, 0))
    gains[...] = jnp.broadcast_to(gain[...], (CH, CH)).T
    biases[...] = jnp.broadcast_to(bias[...], (CH, CH)).T
    weights[...] = weight[...]


def product_other_kernel(core, chunks, total, sent, wide, packed):
    left, rights = operands(chunks, wide, jnp.where(core[0] == 0, 32, 112))
    lane = lax.broadcasted_iota(jnp.int32, (BACK, CH), 1)
    for n in range(4):
        tri = total[pl.ds(n * CH, CH), :] + dot(rights[n].T, left, 1, 0)
        for part, at in enumerate((0, 24, 64, 88)):
            for block in range(8):
                here = tri[at : at + 24, block * CH : (block + 1) * CH]
                tail = here[BACK:]
                tail = jnp.concatenate([pltpu.roll(tail, 96 - 32 * g, 1) for g in range(3)], axis=0)
                chip = n * 4 + part
                rank = rank_of(block, chip // 2, chip % 2)
                packed[pl.ds(rank * BACK, BACK), :] = jnp.where(
                    lane < ROWS, here[:BACK], tail
                )
    sent[...] = packed[...].astype(BF)


def finish_kernel(tri, gate, gain, bias, weight, update, cols, out, done, sems):
    cols[...] = tri[...].astype(F32)
    for row in range(BACK):
        v = cols[pl.ds(row, CH, stride=BACK), :]
        mean = jnp.mean(v, axis=0, keepdims=True)
        centred = v - mean
        var = jnp.mean(centred * centred, axis=0, keepdims=True)
        v = (centred * lax.rsqrt(var + 1e-05) * gain[...] + bias[...]).astype(BF)
        mixed = dot(v, weight[...], 0, 0)
        for start, first, count in ORDER[:5]:
            out[pl.ds(first * COLS + row, count, stride=COLS), :] = mixed[start : start + count]
        group = row // 6
        for start, first, count in ORDER[:5]:
            low, high = max(start, 32 * group), min(start + count, 32 * group + 32)
            if low < high:
                out[pl.ds((first + low - start) * COLS + BACK + row % 6, high - low, stride=COLS), :] = (
                    mixed[ROWS + low - 32 * group : ROWS + high - 32 * group]
                )
    parts = 4
    step = TOKENS // parts
    copies = []
    for part in range(parts):
        here = pl.ds(part * step, step)
        done[here, :] = (gate[here, :] * out[here, :]).astype(BF)
        copies.append(pltpu.make_async_copy(done.at[here, :], update.at[here, :], sems.at[part]))
        copies[-1].start()
    for copy in copies:
        copy.wait()


VMEM = pl.BlockSpec(memory_space=pltpu.VMEM)
SMEM = pl.BlockSpec(memory_space=pltpu.SMEM)
HBM = pl.BlockSpec(memory_space=pltpu.HBM)
PARAMS = pltpu.CompilerParams(vmem_limit_bytes=LIMIT)


def in_hbm(x):
    return pltpu.with_memory_space_constraint(x, pltpu.HBM)


def body(
    pair, pair_mask, in_gain, in_bias, input_proj, gate_weight, out_gain, out_bias, out_weight
):
    sent, normed = pl.pallas_call(
        project_kernel,
        out_shape=(
            pltpu.VMEM((CH * SENT, CH), BF),
            pltpu.VMEM((TOKENS, CH), BF),
        ),
        in_specs=[HBM] * 5,
        out_specs=(VMEM, VMEM),
        scratch_shapes=[
            pltpu.VMEM((TOKENS, CH), BF),
            pltpu.VMEM((COLS, ROWS), jnp.int32),
            pltpu.VMEM((1, CH), F32),
            pltpu.VMEM((1, CH), F32),
            pltpu.VMEM((CH, 4 * CH), BF),
            pltpu.VMEM((TOKENS, CH), F32),
            pltpu.VMEM((CH * SENT, CH), F32),
            pltpu.SemaphoreType.DMA((8,)),
        ],
        compiler_params=PARAMS,
        name="project",
    )(
        in_hbm(pair.reshape(TOKENS, CH)),
        in_hbm(pair_mask.T),
        in_hbm(in_gain.reshape(1, CH)),
        in_hbm(in_bias.reshape(1, CH)),
        in_hbm(input_proj),
    )
    own = lax.all_to_all(sent.reshape(CH, 9, 4, CH), CHIPS, 0, 0, tiled=True)
    other = lax.ppermute(own, "core", [(0, 1), (1, 0)])
    core = lax.axis_index("core").astype(jnp.int32).reshape(1)
    total, gate, gains, biases, weights = pl.pallas_call(
        product_own_kernel,
        out_shape=(
            pltpu.VMEM((4 * CH, 8 * CH), F32),
            pltpu.VMEM((TOKENS, CH), F32),
            pltpu.VMEM((CH, CH), F32),
            pltpu.VMEM((CH, CH), F32),
            pltpu.VMEM((CH, CH), BF),
        ),
        in_specs=[SMEM] + [VMEM] * 6,
        out_specs=[VMEM] * 5,
        scratch_shapes=[pltpu.VMEM((CH * SENT, CH), F32)],
        compiler_params=PARAMS,
        cost_estimate=pl.CostEstimate(flops=4 * 10**8, bytes_accessed=4 * 10**6, transcendentals=0),
        name="product_own",
    )(
        core,
        own.reshape(CH * SENT, CH),
        normed,
        gate_weight,
        out_gain.reshape(1, CH),
        out_bias.reshape(1, CH),
        out_weight,
    )
    tri = pl.pallas_call(
        product_other_kernel,
        out_shape=pltpu.VMEM((CH * BACK, CH), BF),
        in_specs=[SMEM, VMEM, VMEM],
        out_specs=VMEM,
        scratch_shapes=[pltpu.VMEM((CH * SENT, CH), F32), pltpu.VMEM((CH * BACK, CH), F32)],
        compiler_params=PARAMS,
        name="product_other",
    )(core, other.reshape(CH * SENT, CH), total)
    tri = lax.all_to_all(tri.reshape(CH, 9, 2, CH), CHIPS, 0, 0, tiled=True)
    update = pl.pallas_call(
        finish_kernel,
        out_shape=jax.ShapeDtypeStruct((TOKENS, CH), BF),
        in_specs=[VMEM] * 5,
        out_specs=HBM,
        scratch_shapes=[
            pltpu.VMEM((CH * BACK, CH), F32),
            pltpu.VMEM((TOKENS, CH), F32),
            pltpu.VMEM((TOKENS, CH), BF),
            pltpu.SemaphoreType.DMA((4,)),
        ],
        compiler_params=PARAMS,
        name="finish",
    )(tri.reshape(CH * BACK, CH), gate, gains, biases, weights)
    return update.reshape(ROWS, COLS, CH)


def solution(mesh):
    fine = Mesh(mesh.devices.reshape(4, 2, 8, 2, 2), ("y", "xl", "z", "xh", "core"))
    split = P(("y", "xl"), ("z", "xh", "core"))
    return jax.shard_map(
        body,
        mesh=fine,
        in_specs=(split, split, P(), P(), P(), P(), P(), P(), P()),
        out_specs=split,
        check_vma=False,
    )
```

```python
import jax
import jax.numpy as jnp
from jax import lax
from jax.experimental import pallas as pl
from jax.experimental.pallas import tpu as pltpu
from jax.sharding import Mesh
from jax.sharding import PartitionSpec as P

CHIPS = ("xl", "y", "z", "xh")
LIMIT = 48 * 1024 * 1024
ROWS = 96
COLS = 24
CH = 128
SENT = 36
BACK = 18
TOKENS = ROWS * COLS
ORDER = ((0, 56, 16), (16, 24, 24), (40, 72, 24), (64, 0, 24), (88, 48, 8), (96, 0, 24), (120, 48, 8))
BF = jnp.bfloat16
F32 = jnp.float32


def dot(a, b, ca, cb):
    return lax.dot_general(a, b, (((ca,), (cb,)), ((), ())), preferred_element_type=F32)


def sigmoid(v):
    return 0.5 * jnp.tanh(0.5 * v) + 0.5


def project_kernel(
    pair, mask, gain, bias, weight, sent, normed, pair_v, mask_v, gain_v, bias_v, weight_v, rows, out, sems
):
    parts = 1
    step = TOKENS // parts
    here = [pl.ds(part * step, step) for part in range(parts)]
    copies = [
        pltpu.make_async_copy(a, b, sems.at[n])
        for n, (a, b) in enumerate(
            [(mask, mask_v), (weight, weight_v), (gain, gain_v), (bias, bias_v)]
            + [(pair.at[h, :], pair_v.at[h, :]) for h in here]
        )
    ]
    for copy in copies:
        copy.start()
    lane = lax.broadcasted_iota(jnp.int32, (ROWS, CH), 1)
    token = lax.broadcasted_iota(jnp.int32, (ROWS, CH), 0)
    source = lane
    for start, first, count in ORDER:
        source = jnp.where((lane >= start) & (lane < start + count), lane - start + first, source)
    spread = (source == token).astype(F32).astype(BF)
    copies[0].wait()
    copies[1].wait()
    half_live = 0.5 * dot(mask_v[...].astype(F32).astype(BF), spread, 1, 0)
    turned = weight_v[...].astype(F32).T
    turned = jnp.concatenate(
        [turned[n * CH : (n + 1) * CH] * (1.0 if n % 2 else 0.5) for n in range(4)], axis=0
    ).astype(BF)
    at_lane = lax.broadcasted_iota(jnp.int32, (CH, CH), 1)

    copies[2].wait()
    copies[3].wait()
    for part in range(parts):
        copies[4 + part].wait()
        for at in range(part * step, (part + 1) * step, 192):
            x = pair_v[pl.ds(at, 192), :].astype(F32)
            mean = jnp.mean(x, axis=-1, keepdims=True)
            centred = x - mean
            var = jnp.mean(centred * centred, axis=-1, keepdims=True)
            x = centred * lax.rsqrt(var + 1e-05) * gain_v[...] + bias_v[...]
            normed[pl.ds(at, 192), :] = x.astype(BF)
            rows[pl.ds(at, 192), :] = x

    def column(k):
        x = rows[pl.ds(k, ROWS, stride=COLS), :]
        x = jnp.concatenate([x[first : first + count] for _, first, count in ORDER], axis=0)
        x = x.astype(BF)
        proj = dot(turned, x, 1, 1)
        m = half_live[k : k + 1, :]
        left = (m * jnp.tanh(proj[:CH]) + m) * proj[CH : 2 * CH]
        right = (m * jnp.tanh(proj[2 * CH : 3 * CH]) + m) * proj[3 * CH :]
        out[pl.ds(k, CH, stride=SENT), :] = jnp.where(at_lane < ROWS, left, right)
        return right

    for k in range(12):
        low = column(k)
        high = column(k + 12)
        out[pl.ds(24 + k, CH, stride=SENT), :] = jnp.where(
            at_lane < 64, low, pltpu.roll(high, 64, 1)
        )
    sent[...] = out[...].astype(BF)


SIZES = {"y": 4, "xl": 2, "z": 8, "xh": 2}
STEP, span = {}, 1
for axis in reversed(CHIPS):
    STEP[axis], span = span, span * SIZES[axis]


def rank_of(block, z, xh):
    return block // 2 * STEP["y"] + block % 2 * STEP["xl"] + z * STEP["z"] + xh * STEP["xh"]


def operands(chunks, wide, core):
    wide[...] = chunks[...].astype(F32)
    shifts = jnp.where(core == 0, 32, 112), jnp.where(core == 0, 96, 48)
    lane = lax.broadcasted_iota(jnp.int32, (384, CH), 1)
    lefts, rights = [], []
    for block in range(8):
        starts = [rank_of(block, 0, xh) * SENT for xh in range(2)]

        def gather(ks):
            return jnp.concatenate(
                [wide[pl.ds(at + k, 8, stride=SENT * STEP["z"]), :] for k in ks for at in starts],
                axis=0,
            )

        left = gather(range(24))
        mid = gather(range(24, SENT))
        right = jnp.concatenate([mid, pltpu.roll(mid, 64, 1)], axis=0)
        right = jnp.where(lane < 64, right, left)
        rights.append(pltpu.roll(right, shifts[block % 2], 1))
        lefts.append(left.astype(BF))
    pairs = [
        jnp.where(lane < 64, rights[2 * n], rights[2 * n + 1]).astype(BF)
        for n in range(4)
    ]
    return jnp.concatenate(lefts, axis=1), pairs


def product_own_kernel(
    core, chunks, normed, gate_weight, gain, bias, weight, total, gate, gains, biases, weights, wide
):
    left, rights = operands(chunks, wide, core[0])
    for n in range(4):
        total[pl.ds(n * CH, CH), :] = dot(rights[n].T, left, 1, 0)
    for at in range(0, TOKENS, 256):
        here = pl.ds(at, 256)
        gate[here, :] = sigmoid(dot(normed[here, :], gate_weight[...], 1, 0))
    gains[...] = jnp.broadcast_to(gain[...], (CH, CH)).T
    biases[...] = jnp.broadcast_to(bias[...], (CH, CH)).T
    weights[...] = weight[...]


def product_other_kernel(core, chunks, total, sent, wide, packed):
    left, rights = operands(chunks, wide, core[0])
    lane = lax.broadcasted_iota(jnp.int32, (BACK, CH), 1)
    for n in range(4):
        tri = total[pl.ds(n * CH, CH), :] + dot(rights[n].T, left, 1, 0)
        for part, at in enumerate((0, 24, 64, 88)):
            for block in range(8):
                here = tri[at : at + 24, block * CH : (block + 1) * CH]
                tail = here[BACK:]
                tail = jnp.concatenate([pltpu.roll(tail, 96 - 32 * g, 1) for g in range(3)], axis=0)
                chip = n * 4 + part
                rank = rank_of(block, chip // 2, chip % 2)
                packed[pl.ds(rank * BACK, BACK), :] = jnp.where(
                    lane < ROWS, here[:BACK], tail
                )
    sent[...] = packed[pl.ds(0, CH * BACK), :].astype(BF)


def finish_kernel(tri, gate, gain, bias, weight, update, cols, out, done, sems):
    cols[...] = tri[...].astype(F32)
    for row in range(BACK):
        v = cols[pl.ds(row, CH, stride=BACK), :]
        mean = jnp.mean(v, axis=0, keepdims=True)
        centred = v - mean
        var = jnp.mean(centred * centred, axis=0, keepdims=True)
        v = (centred * lax.rsqrt(var + 1e-05) * gain[...] + bias[...]).astype(BF)
        mixed = dot(v, weight[...], 0, 0)
        for start, first, count in ORDER[:5]:
            out[pl.ds(first * COLS + row, count, stride=COLS), :] = mixed[start : start + count]
        group = row // 6
        for start, first, count in ORDER[:5]:
            low, high = max(start, 32 * group), min(start + count, 32 * group + 32)
            if low < high:
                out[pl.ds((first + low - start) * COLS + BACK + row % 6, high - low, stride=COLS), :] = (
                    mixed[ROWS + low - 32 * group : ROWS + high - 32 * group]
                )
    parts = 4
    step = TOKENS // parts
    copies = []
    for part in range(parts):
        here = pl.ds(part * step, step)
        done[here, :] = (gate[here, :] * out[here, :]).astype(BF)
        copies.append(pltpu.make_async_copy(done.at[here, :], update.at[here, :], sems.at[part]))
        copies[-1].start()
    for copy in copies:
        copy.wait()


VMEM = pl.BlockSpec(memory_space=pltpu.VMEM)
SMEM = pl.BlockSpec(memory_space=pltpu.SMEM)
HBM = pl.BlockSpec(memory_space=pltpu.HBM)
PARAMS = pltpu.CompilerParams(vmem_limit_bytes=LIMIT)


def in_hbm(x):
    return pltpu.with_memory_space_constraint(x, pltpu.HBM)


def body(
    pair, pair_mask, in_gain, in_bias, input_proj, gate_weight, out_gain, out_bias, out_weight
):
    sent, normed = pl.pallas_call(
        project_kernel,
        out_shape=(
            pltpu.VMEM((CH * SENT, CH), BF),
            pltpu.VMEM((TOKENS, CH), BF),
        ),
        in_specs=[HBM] * 5,
        out_specs=(VMEM, VMEM),
        scratch_shapes=[
            pltpu.VMEM((TOKENS, CH), BF),
            pltpu.VMEM((COLS, ROWS), jnp.int32),
            pltpu.VMEM((1, CH), F32),
            pltpu.VMEM((1, CH), F32),
            pltpu.VMEM((CH, 4 * CH), BF),
            pltpu.VMEM((TOKENS, CH), F32),
            pltpu.VMEM((CH * SENT, CH), F32),
            pltpu.SemaphoreType.DMA((8,)),
        ],
        compiler_params=PARAMS,
        name="project",
    )(
        in_hbm(pair.reshape(TOKENS, CH)),
        in_hbm(pair_mask.T),
        in_hbm(in_gain.reshape(1, CH)),
        in_hbm(in_bias.reshape(1, CH)),
        in_hbm(input_proj),
    )
    own = lax.all_to_all(sent.reshape(CH, 9, 4, CH), CHIPS, 0, 0, tiled=True)
    other = lax.ppermute(own, "core", [(0, 1), (1, 0)])
    core = lax.axis_index("core").astype(jnp.int32).reshape(1)
    total, gate, gains, biases, weights = pl.pallas_call(
        product_own_kernel,
        out_shape=(
            pltpu.VMEM((4 * CH, 8 * CH), F32),
            pltpu.VMEM((TOKENS, CH), F32),
            pltpu.VMEM((CH, CH), F32),
            pltpu.VMEM((CH, CH), F32),
            pltpu.VMEM((CH, CH), BF),
        ),
        in_specs=[SMEM] + [VMEM] * 6,
        out_specs=[VMEM] * 5,
        scratch_shapes=[pltpu.VMEM((CH * SENT, CH), F32)],
        compiler_params=PARAMS,
        cost_estimate=pl.CostEstimate(flops=4 * 10**8, bytes_accessed=4 * 10**6, transcendentals=0),
        name="product_own",
    )(
        core,
        own.reshape(CH * SENT, CH),
        normed,
        gate_weight,
        out_gain.reshape(1, CH),
        out_bias.reshape(1, CH),
        out_weight,
    )
    tri = pl.pallas_call(
        product_other_kernel,
        out_shape=pltpu.VMEM((CH * BACK, CH), BF),
        in_specs=[SMEM, VMEM, VMEM],
        out_specs=VMEM,
        scratch_shapes=[pltpu.VMEM((CH * SENT, CH), F32), pltpu.VMEM((CH * BACK + 8, CH), F32)],
        compiler_params=PARAMS,
        name="product_other",
    )(core, other.reshape(CH * SENT, CH), total)
    tri = lax.all_to_all(tri.reshape(CH, 9, 2, CH), CHIPS, 0, 0, tiled=True)
    update = pl.pallas_call(
        finish_kernel,
        out_shape=jax.ShapeDtypeStruct((TOKENS, CH), BF),
        in_specs=[VMEM] * 5,
        out_specs=HBM,
        scratch_shapes=[
            pltpu.VMEM((CH * BACK, CH), F32),
            pltpu.VMEM((TOKENS, CH), F32),
            pltpu.VMEM((TOKENS, CH), BF),
            pltpu.SemaphoreType.DMA((4,)),
        ],
        compiler_params=PARAMS,
        name="finish",
    )(tri.reshape(CH * BACK, CH), gate, gains, biases, weights)
    return update.reshape(ROWS, COLS, CH)


def solution(mesh):
    fine = Mesh(mesh.devices.reshape(4, 2, 8, 2, 2), ("y", "xl", "z", "xh", "core"))
    split = P(("y", "xl"), ("z", "xh", "core"))
    return jax.shard_map(
        body,
        mesh=fine,
        in_specs=(split, split, P(), P(), P(), P(), P(), P(), P()),
        out_specs=split,
        check_vma=False,
    )
```

```python
import jax
import jax.numpy as jnp
from jax import lax
from jax.experimental import pallas as pl
from jax.experimental.pallas import tpu as pltpu
from jax.sharding import Mesh
from jax.sharding import PartitionSpec as P

OUTWARD = ("y", "xl", "z", "xh")
HOMEWARD = ("xl", "y", "z", "xh")
LIMIT = 48 * 1024 * 1024
ROWS = 96
COLS = 24
CH = 128
SENT = 36
BACK = 18
TOKENS = ROWS * COLS
ORDER = ((0, 56, 16), (16, 24, 24), (40, 72, 24), (64, 0, 24), (88, 48, 8), (96, 0, 24), (120, 48, 8))
BF = jnp.bfloat16
F32 = jnp.float32


def dot(a, b, ca, cb):
    return lax.dot_general(a, b, (((ca,), (cb,)), ((), ())), preferred_element_type=F32)


def sigmoid(v):
    return 0.5 * jnp.tanh(0.5 * v) + 0.5


def project_kernel(
    pair, mask, gain, bias, weight, sent, normed, pair_v, mask_v, gain_v, bias_v, weight_v, rows, out, sems
):
    parts = 1
    step = TOKENS // parts
    here = [pl.ds(part * step, step) for part in range(parts)]
    copies = [
        pltpu.make_async_copy(a, b, sems.at[n])
        for n, (a, b) in enumerate(
            [(mask, mask_v), (weight, weight_v), (gain, gain_v), (bias, bias_v)]
            + [(pair.at[h, :], pair_v.at[h, :]) for h in here]
        )
    ]
    for copy in copies:
        copy.start()
    lane = lax.broadcasted_iota(jnp.int32, (ROWS, CH), 1)
    token = lax.broadcasted_iota(jnp.int32, (ROWS, CH), 0)
    source = lane
    for start, first, count in ORDER:
        source = jnp.where((lane >= start) & (lane < start + count), lane - start + first, source)
    spread = (source == token).astype(F32).astype(BF)
    copies[0].wait()
    copies[1].wait()
    half_live = 0.5 * dot(mask_v[...].astype(F32).astype(BF), spread, 1, 0)
    turned = weight_v[...].astype(F32).T
    turned = jnp.concatenate(
        [turned[n * CH : (n + 1) * CH] * (1.0 if n % 2 else 0.5) for n in range(4)], axis=0
    ).astype(BF)
    at_lane = lax.broadcasted_iota(jnp.int32, (CH, CH), 1)

    copies[2].wait()
    copies[3].wait()
    for part in range(parts):
        copies[4 + part].wait()
        for at in range(part * step, (part + 1) * step, 192):
            x = pair_v[pl.ds(at, 192), :].astype(F32)
            mean = jnp.mean(x, axis=-1, keepdims=True)
            centred = x - mean
            var = jnp.mean(centred * centred, axis=-1, keepdims=True)
            x = centred * lax.rsqrt(var + 1e-05) * gain_v[...] + bias_v[...]
            normed[pl.ds(at, 192), :] = x.astype(BF)
            rows[pl.ds(at, 192), :] = x

    def column(k):
        x = rows[pl.ds(k, ROWS, stride=COLS), :]
        x = jnp.concatenate([x[first : first + count] for _, first, count in ORDER], axis=0)
        x = x.astype(BF)
        proj = dot(turned, x, 1, 1)
        m = half_live[k : k + 1, :]
        left = (m * jnp.tanh(proj[:CH]) + m) * proj[CH : 2 * CH]
        right = (m * jnp.tanh(proj[2 * CH : 3 * CH]) + m) * proj[3 * CH :]
        out[pl.ds(k, CH, stride=SENT), :] = jnp.where(at_lane < ROWS, left, right)
        return right

    for k in range(12):
        low = column(k)
        high = column(k + 12)
        out[pl.ds(24 + k, CH, stride=SENT), :] = jnp.where(
            at_lane < 64, low, pltpu.roll(high, 64, 1)
        )
    sent[...] = out[pl.ds(0, CH * SENT), :].astype(BF)


SIZES = {"y": 4, "xl": 2, "z": 8, "xh": 2}


def rank_of(order, block, z, xh):
    rank = 0
    for axis in order:
        rank = rank * SIZES[axis] + {"y": block // 2, "xl": block % 2, "z": z, "xh": xh}[axis]
    return rank


STEP = rank_of(OUTWARD, 0, 1, 0)


def homeward_rows(values):
    blocks = sorted(range(8), key=lambda block: rank_of(HOMEWARD, block, 0, 0))
    starts = [rank_of(OUTWARD, block, 0, 0) for block in blocks]
    return jnp.concatenate([values[at : at + 16] for at in starts], axis=0)


def operands(chunks, wide, core):
    wide[pl.ds(0, CH * SENT), :] = chunks[...].astype(F32)
    shifts = jnp.where(core == 0, 32, 112), jnp.where(core == 0, 96, 48)
    lane = lax.broadcasted_iota(jnp.int32, (384, CH), 1)
    lefts, rights = [], []
    for block in range(8):
        starts = [rank_of(OUTWARD, block, 0, xh) * SENT for xh in range(2)]

        def gather(ks):
            return jnp.concatenate(
                [wide[pl.ds(at + k, 8, stride=SENT * STEP), :] for k in ks for at in starts],
                axis=0,
            )

        left = gather(range(24))
        mid = gather(range(24, SENT))
        right = jnp.concatenate([mid, pltpu.roll(mid, 64, 1)], axis=0)
        right = jnp.where(lane < 64, right, left)
        rights.append(pltpu.roll(right, shifts[block % 2], 1))
        lefts.append(left.astype(BF))
    pairs = [
        jnp.where(lane < 64, rights[2 * n], rights[2 * n + 1]).astype(BF)
        for n in range(4)
    ]
    return jnp.concatenate(lefts, axis=1), pairs


def product_own_kernel(
    core, chunks, normed, gate_weight, gain, bias, weight, total, gate, gains, biases, weights, wide
):
    left, rights = operands(chunks, wide, core[0])
    for n in range(4):
        total[pl.ds(n * CH, CH), :] = dot(rights[n].T, left, 1, 0)
    for at in range(0, TOKENS, 256):
        here = pl.ds(at, 256)
        gate[here, :] = sigmoid(dot(normed[here, :], gate_weight[...], 1, 0))
    gains[...] = homeward_rows(jnp.broadcast_to(gain[...], (CH, CH)).T)
    biases[...] = homeward_rows(jnp.broadcast_to(bias[...], (CH, CH)).T)
    weights[...] = homeward_rows(weight[...])


def product_other_kernel(core, chunks, total, sent, wide, packed):
    left, rights = operands(chunks, wide, core[0])
    lane = lax.broadcasted_iota(jnp.int32, (BACK, CH), 1)
    for n in range(4):
        tri = total[pl.ds(n * CH, CH), :] + dot(rights[n].T, left, 1, 0)
        for part, at in enumerate((0, 24, 64, 88)):
            for block in range(8):
                here = tri[at : at + 24, block * CH : (block + 1) * CH]
                tail = here[BACK:]
                tail = jnp.concatenate([pltpu.roll(tail, 96 - 32 * g, 1) for g in range(3)], axis=0)
                chip = n * 4 + part
                rank = rank_of(HOMEWARD, block, chip // 2, chip % 2)
                packed[pl.ds(rank * BACK, BACK), :] = jnp.where(
                    lane < ROWS, here[:BACK], tail
                )
    sent[...] = packed[pl.ds(0, CH * BACK), :].astype(BF)


def finish_kernel(tri, gate, gain, bias, weight, update, cols, out, done, sems):
    cols[pl.ds(0, CH * BACK), :] = tri[...].astype(F32)
    for row in range(BACK):
        v = cols[pl.ds(row, CH, stride=BACK), :]
        mean = jnp.mean(v, axis=0, keepdims=True)
        centred = v - mean
        var = jnp.mean(centred * centred, axis=0, keepdims=True)
        v = (centred * lax.rsqrt(var + 1e-05) * gain[...] + bias[...]).astype(BF)
        mixed = dot(v, weight[...], 0, 0)
        for start, first, count in ORDER[:5]:
            out[pl.ds(first * COLS + row, count, stride=COLS), :] = mixed[start : start + count]
        group = row // 6
        for start, first, count in ORDER[:5]:
            low, high = max(start, 32 * group), min(start + count, 32 * group + 32)
            if low < high:
                out[pl.ds((first + low - start) * COLS + BACK + row % 6, high - low, stride=COLS), :] = (
                    mixed[ROWS + low - 32 * group : ROWS + high - 32 * group]
                )
    parts = 4
    step = TOKENS // parts
    copies = []
    for part in range(parts):
        here = pl.ds(part * step, step)
        done[here, :] = (gate[here, :] * out[here, :]).astype(BF)
        copies.append(pltpu.make_async_copy(done.at[here, :], update.at[here, :], sems.at[part]))
        copies[-1].start()
    for copy in copies:
        copy.wait()


VMEM = pl.BlockSpec(memory_space=pltpu.VMEM)
SMEM = pl.BlockSpec(memory_space=pltpu.SMEM)
HBM = pl.BlockSpec(memory_space=pltpu.HBM)
PARAMS = pltpu.CompilerParams(vmem_limit_bytes=LIMIT)


def in_hbm(x):
    return pltpu.with_memory_space_constraint(x, pltpu.HBM)


def body(
    pair, pair_mask, in_gain, in_bias, input_proj, gate_weight, out_gain, out_bias, out_weight
):
    sent, normed = pl.pallas_call(
        project_kernel,
        out_shape=(
            pltpu.VMEM((CH * SENT, CH), BF),
            pltpu.VMEM((TOKENS, CH), BF),
        ),
        in_specs=[HBM] * 5,
        out_specs=(VMEM, VMEM),
        scratch_shapes=[
            pltpu.VMEM((TOKENS, CH), BF),
            pltpu.VMEM((COLS, ROWS), jnp.int32),
            pltpu.VMEM((1, CH), F32),
            pltpu.VMEM((1, CH), F32),
            pltpu.VMEM((CH, 4 * CH), BF),
            pltpu.VMEM((TOKENS + COLS, CH), F32),
            pltpu.VMEM((CH * SENT + SENT, CH), F32),
            pltpu.SemaphoreType.DMA((8,)),
        ],
        compiler_params=PARAMS,
        name="project",
    )(
        in_hbm(pair.reshape(TOKENS, CH)),
        in_hbm(pair_mask.T),
        in_hbm(in_gain.reshape(1, CH)),
        in_hbm(in_bias.reshape(1, CH)),
        in_hbm(input_proj),
    )
    own = lax.all_to_all(sent.reshape(CH, 9, 4, CH), OUTWARD, 0, 0, tiled=True)
    other = lax.ppermute(own, "core", [(0, 1), (1, 0)])
    core = lax.axis_index("core").astype(jnp.int32).reshape(1)
    total, gate, gains, biases, weights = pl.pallas_call(
        product_own_kernel,
        out_shape=(
            pltpu.VMEM((4 * CH, 8 * CH), F32),
            pltpu.VMEM((TOKENS, CH), F32),
            pltpu.VMEM((CH, CH), F32),
            pltpu.VMEM((CH, CH), F32),
            pltpu.VMEM((CH, CH), BF),
        ),
        in_specs=[SMEM] + [VMEM] * 6,
        out_specs=[VMEM] * 5,
        scratch_shapes=[pltpu.VMEM((CH * SENT + STEP * SENT, CH), F32)],
        compiler_params=PARAMS,
        cost_estimate=pl.CostEstimate(flops=4 * 10**8, bytes_accessed=4 * 10**6, transcendentals=0),
        name="product_own",
    )(
        core,
        own.reshape(CH * SENT, CH),
        normed,
        gate_weight,
        out_gain.reshape(1, CH),
        out_bias.reshape(1, CH),
        out_weight,
    )
    tri = pl.pallas_call(
        product_other_kernel,
        out_shape=pltpu.VMEM((CH * BACK, CH), BF),
        in_specs=[SMEM, VMEM, VMEM],
        out_specs=VMEM,
        scratch_shapes=[
            pltpu.VMEM((CH * SENT + STEP * SENT, CH), F32),
            pltpu.VMEM((CH * BACK + 8, CH), F32),
        ],
        compiler_params=PARAMS,
        name="product_other",
    )(core, other.reshape(CH * SENT, CH), total)
    tri = lax.all_to_all(tri.reshape(CH, 9, 2, CH), HOMEWARD, 0, 0, tiled=True)
    update = pl.pallas_call(
        finish_kernel,
        out_shape=jax.ShapeDtypeStruct((TOKENS, CH), BF),
        in_specs=[VMEM] * 5,
        out_specs=HBM,
        scratch_shapes=[
            pltpu.VMEM((CH * BACK + BACK, CH), F32),
            pltpu.VMEM((TOKENS + COLS, CH), F32),
            pltpu.VMEM((TOKENS, CH), BF),
            pltpu.SemaphoreType.DMA((4,)),
        ],
        compiler_params=PARAMS,
        name="finish",
    )(tri.reshape(CH * BACK, CH), gate, gains, biases, weights)
    return update.reshape(ROWS, COLS, CH)


def solution(mesh):
    fine = Mesh(mesh.devices.reshape(4, 2, 8, 2, 2), ("y", "xl", "z", "xh", "core"))
    split = P(("y", "xl"), ("z", "xh", "core"))
    return jax.shard_map(
        body,
        mesh=fine,
        in_specs=(split, split, P(), P(), P(), P(), P(), P(), P()),
        out_specs=split,
        check_vma=False,
    )
```

```python
import jax
import jax.numpy as jnp
from jax import lax
from jax.experimental import pallas as pl
from jax.experimental.pallas import tpu as pltpu
from jax.sharding import Mesh
from jax.sharding import PartitionSpec as P

OUTWARD = ("y", "xl", "z", "xh")
HOMEWARD = ("xl", "y", "z", "xh")
LIMIT = 48 * 1024 * 1024
ROWS = 96
COLS = 24
CH = 128
SENT = 36
BACK = 18
TOKENS = ROWS * COLS
ORDER = ((0, 56, 16), (16, 24, 24), (40, 72, 24), (64, 0, 24), (88, 48, 8), (96, 0, 24), (120, 48, 8))
BF = jnp.bfloat16
F32 = jnp.float32


def dot(a, b, ca, cb):
    return lax.dot_general(a, b, (((ca,), (cb,)), ((), ())), preferred_element_type=F32)


def sigmoid(v):
    return 0.5 * jnp.tanh(0.5 * v) + 0.5


def project_kernel(
    pair, mask, gain, bias, weight, sent, normed, pair_v, mask_v, gain_v, bias_v, weight_v, rows, out, sems
):
    parts = 1
    step = TOKENS // parts
    here = [pl.ds(part * step, step) for part in range(parts)]
    copies = [
        pltpu.make_async_copy(a, b, sems.at[n])
        for n, (a, b) in enumerate(
            [(mask, mask_v), (weight, weight_v), (gain, gain_v), (bias, bias_v)]
            + [(pair.at[h, :], pair_v.at[h, :]) for h in here]
        )
    ]
    for copy in copies:
        copy.start()
    lane = lax.broadcasted_iota(jnp.int32, (ROWS, CH), 1)
    token = lax.broadcasted_iota(jnp.int32, (ROWS, CH), 0)
    source = lane
    for start, first, count in ORDER:
        source = jnp.where((lane >= start) & (lane < start + count), lane - start + first, source)
    spread = (source == token).astype(F32).astype(BF)
    copies[0].wait()
    copies[1].wait()
    half_live = 0.5 * dot(mask_v[...].astype(F32).astype(BF), spread, 1, 0)
    turned = weight_v[...].astype(F32).T
    turned = jnp.concatenate(
        [turned[n * CH : (n + 1) * CH] * (1.0 if n % 2 else 0.5) for n in range(4)], axis=0
    ).astype(BF)
    at_lane = lax.broadcasted_iota(jnp.int32, (CH, CH), 1)

    copies[2].wait()
    copies[3].wait()
    for part in range(parts):
        copies[4 + part].wait()
        for at in range(part * step, (part + 1) * step, 192):
            x = pair_v[pl.ds(at, 192), :].astype(F32)
            mean = jnp.mean(x, axis=-1, keepdims=True)
            centred = x - mean
            var = jnp.mean(centred * centred, axis=-1, keepdims=True)
            x = centred * lax.rsqrt(var + 1e-05) * gain_v[...] + bias_v[...]
            normed[pl.ds(at, 192), :] = x.astype(BF)
            rows[pl.ds(at, 192), :] = x

    def column(k):
        x = rows[pl.ds(k, ROWS, stride=COLS), :]
        x = jnp.concatenate([x[first : first + count] for _, first, count in ORDER], axis=0)
        x = x.astype(BF)
        proj = dot(turned, x, 1, 1)
        m = half_live[k : k + 1, :]
        left = (m * jnp.tanh(proj[:CH]) + m) * proj[CH : 2 * CH]
        right = (m * jnp.tanh(proj[2 * CH : 3 * CH]) + m) * proj[3 * CH :]
        out[pl.ds(k, CH, stride=SENT), :] = jnp.where(at_lane < ROWS, left, right)
        return right

    for k in range(12):
        low = column(k)
        high = column(k + 12)
        out[pl.ds(24 + k, CH, stride=SENT), :] = jnp.where(
            at_lane < 64, low, pltpu.roll(high, 64, 1)
        )
    sent[...] = out[pl.ds(0, CH * SENT), :].astype(BF)


SIZES = {"y": 4, "xl": 2, "z": 8, "xh": 2}


def rank_of(order, block, z, xh):
    rank = 0
    for axis in order:
        rank = rank * SIZES[axis] + {"y": block // 2, "xl": block % 2, "z": z, "xh": xh}[axis]
    return rank


STEP = rank_of(OUTWARD, 0, 1, 0)


def homeward_rows(values):
    blocks = sorted(range(8), key=lambda block: rank_of(HOMEWARD, block, 0, 0))
    starts = [rank_of(OUTWARD, block, 0, 0) for block in blocks]
    return jnp.concatenate([values[at : at + 16] for at in starts], axis=0)


def operands(chunks, wide, core, blocks=range(8)):
    base = rank_of(OUTWARD, blocks[0], 0, 0)
    wide[pl.ds(0, len(blocks) * 16 * SENT), :] = chunks[...].astype(F32)
    shifts = jnp.where(core == 0, 32, 112), jnp.where(core == 0, 96, 48)
    lane = lax.broadcasted_iota(jnp.int32, (384, CH), 1)
    lefts, rights = [], []
    for block in blocks:
        starts = [(rank_of(OUTWARD, block, 0, xh) - base) * SENT for xh in range(2)]

        def gather(ks):
            return jnp.concatenate(
                [wide[pl.ds(at + k, 8, stride=SENT * STEP), :] for k in ks for at in starts],
                axis=0,
            )

        left = gather(range(24))
        mid = gather(range(24, SENT))
        right = jnp.concatenate([mid, pltpu.roll(mid, 64, 1)], axis=0)
        right = jnp.where(lane < 64, right, left)
        rights.append(pltpu.roll(right, shifts[block % 2], 1))
        lefts.append(left.astype(BF))
    pairs = [
        jnp.where(lane < 64, rights[2 * n], rights[2 * n + 1]).astype(BF)
        for n in range(len(blocks) // 2)
    ]
    return jnp.concatenate(lefts, axis=1), pairs


def product_own_kernel(
    core, chunks, normed, gate_weight, gain, bias, weight, total, gate, gains, biases, weights, wide
):
    left, rights = operands(chunks, wide, core[0])
    for n in range(4):
        total[pl.ds(n * CH, CH), :] = dot(rights[n].T, left, 1, 0)
    for at in range(0, TOKENS, 256):
        here = pl.ds(at, 256)
        gate[here, :] = sigmoid(dot(normed[here, :], gate_weight[...], 1, 0))
    gains[...] = homeward_rows(jnp.broadcast_to(gain[...], (CH, CH)).T)
    biases[...] = homeward_rows(jnp.broadcast_to(bias[...], (CH, CH)).T)
    weights[...] = homeward_rows(weight[...])


def prepare_kernel(core, chunks, left, right, wide):
    lefts, rights = operands(chunks, wide, core[0], range(4))
    left[...] = lefts
    for n in range(2):
        right[n] = rights[n]


def product_other_kernel(core, chunks, left_first, right_first, total, sent, wide, packed):
    left, rights = operands(chunks, wide, core[0], range(4, 8))
    left = jnp.concatenate([left_first[...], left], axis=1)
    rights = [right_first[0], right_first[1]] + rights
    lane = lax.broadcasted_iota(jnp.int32, (BACK, CH), 1)
    for n in range(4):
        tri = total[pl.ds(n * CH, CH), :] + dot(rights[n].T, left, 1, 0)
        for part, at in enumerate((0, 24, 64, 88)):
            for block in range(8):
                here = tri[at : at + 24, block * CH : (block + 1) * CH]
                tail = here[BACK:]
                tail = jnp.concatenate([pltpu.roll(tail, 96 - 32 * g, 1) for g in range(3)], axis=0)
                chip = n * 4 + part
                rank = rank_of(HOMEWARD, block, chip // 2, chip % 2)
                packed[pl.ds(rank * BACK, BACK), :] = jnp.where(
                    lane < ROWS, here[:BACK], tail
                )
    sent[...] = packed[pl.ds(0, CH * BACK), :].astype(BF)


def finish_kernel(tri, gate, gain, bias, weight, update, cols, out, done, sems):
    cols[pl.ds(0, CH * BACK), :] = tri[...].astype(F32)
    for row in range(BACK):
        v = cols[pl.ds(row, CH, stride=BACK), :]
        mean = jnp.mean(v, axis=0, keepdims=True)
        centred = v - mean
        var = jnp.mean(centred * centred, axis=0, keepdims=True)
        v = (centred * lax.rsqrt(var + 1e-05) * gain[...] + bias[...]).astype(BF)
        mixed = dot(v, weight[...], 0, 0)
        for start, first, count in ORDER[:5]:
            out[pl.ds(first * COLS + row, count, stride=COLS), :] = mixed[start : start + count]
        group = row // 6
        for start, first, count in ORDER[:5]:
            low, high = max(start, 32 * group), min(start + count, 32 * group + 32)
            if low < high:
                out[pl.ds((first + low - start) * COLS + BACK + row % 6, high - low, stride=COLS), :] = (
                    mixed[ROWS + low - 32 * group : ROWS + high - 32 * group]
                )
    parts = 4
    step = TOKENS // parts
    copies = []
    for part in range(parts):
        here = pl.ds(part * step, step)
        done[here, :] = (gate[here, :] * out[here, :]).astype(BF)
        copies.append(pltpu.make_async_copy(done.at[here, :], update.at[here, :], sems.at[part]))
        copies[-1].start()
    for copy in copies:
        copy.wait()


VMEM = pl.BlockSpec(memory_space=pltpu.VMEM)
SMEM = pl.BlockSpec(memory_space=pltpu.SMEM)
HBM = pl.BlockSpec(memory_space=pltpu.HBM)
PARAMS = pltpu.CompilerParams(vmem_limit_bytes=LIMIT)


def in_hbm(x):
    return pltpu.with_memory_space_constraint(x, pltpu.HBM)


def body(
    pair, pair_mask, in_gain, in_bias, input_proj, gate_weight, out_gain, out_bias, out_weight
):
    sent, normed = pl.pallas_call(
        project_kernel,
        out_shape=(
            pltpu.VMEM((CH * SENT, CH), BF),
            pltpu.VMEM((TOKENS, CH), BF),
        ),
        in_specs=[HBM] * 5,
        out_specs=(VMEM, VMEM),
        scratch_shapes=[
            pltpu.VMEM((TOKENS, CH), BF),
            pltpu.VMEM((COLS, ROWS), jnp.int32),
            pltpu.VMEM((1, CH), F32),
            pltpu.VMEM((1, CH), F32),
            pltpu.VMEM((CH, 4 * CH), BF),
            pltpu.VMEM((TOKENS + COLS, CH), F32),
            pltpu.VMEM((CH * SENT + SENT, CH), F32),
            pltpu.SemaphoreType.DMA((8,)),
        ],
        compiler_params=PARAMS,
        name="project",
    )(
        in_hbm(pair.reshape(TOKENS, CH)),
        in_hbm(pair_mask.T),
        in_hbm(in_gain.reshape(1, CH)),
        in_hbm(in_bias.reshape(1, CH)),
        in_hbm(input_proj),
    )
    own = lax.all_to_all(sent.reshape(CH, 9, 4, CH), OUTWARD, 0, 0, tiled=True)
    swap = [(0, 1), (1, 0)]
    other_first = lax.ppermute(own[: CH // 2], "core", swap)
    other_last = lax.ppermute(own[CH // 2 :], "core", swap)
    core = lax.axis_index("core").astype(jnp.int32).reshape(1)
    total, gate, gains, biases, weights = pl.pallas_call(
        product_own_kernel,
        out_shape=(
            pltpu.VMEM((4 * CH, 8 * CH), F32),
            pltpu.VMEM((TOKENS, CH), F32),
            pltpu.VMEM((CH, CH), F32),
            pltpu.VMEM((CH, CH), F32),
            pltpu.VMEM((CH, CH), BF),
        ),
        in_specs=[SMEM] + [VMEM] * 6,
        out_specs=[VMEM] * 5,
        scratch_shapes=[pltpu.VMEM((CH * SENT + STEP * SENT, CH), F32)],
        compiler_params=PARAMS,
        cost_estimate=pl.CostEstimate(flops=4 * 10**8, bytes_accessed=4 * 10**6, transcendentals=0),
        name="product_own",
    )(
        core,
        own.reshape(CH * SENT, CH),
        normed,
        gate_weight,
        out_gain.reshape(1, CH),
        out_bias.reshape(1, CH),
        out_weight,
    )
    half = CH // 2 * SENT
    left_first, right_first = pl.pallas_call(
        prepare_kernel,
        out_shape=(pltpu.VMEM((384, 4 * CH), BF), pltpu.VMEM((2, 384, CH), BF)),
        in_specs=[SMEM, VMEM],
        out_specs=[VMEM] * 2,
        scratch_shapes=[pltpu.VMEM((half + STEP * SENT, CH), F32)],
        compiler_params=PARAMS,
        cost_estimate=pl.CostEstimate(flops=10**8, bytes_accessed=2 * 10**6, transcendentals=0),
        name="prepare",
    )(core, other_first.reshape(half, CH))
    tri = pl.pallas_call(
        product_other_kernel,
        out_shape=pltpu.VMEM((CH * BACK, CH), BF),
        in_specs=[SMEM] + [VMEM] * 4,
        out_specs=VMEM,
        scratch_shapes=[
            pltpu.VMEM((half + STEP * SENT, CH), F32),
            pltpu.VMEM((CH * BACK + 8, CH), F32),
        ],
        compiler_params=PARAMS,
        name="product_other",
    )(core, other_last.reshape(half, CH), left_first, right_first, total)
    tri = lax.all_to_all(tri.reshape(CH, 9, 2, CH), HOMEWARD, 0, 0, tiled=True)
    update = pl.pallas_call(
        finish_kernel,
        out_shape=jax.ShapeDtypeStruct((TOKENS, CH), BF),
        in_specs=[VMEM] * 5,
        out_specs=HBM,
        scratch_shapes=[
            pltpu.VMEM((CH * BACK + BACK, CH), F32),
            pltpu.VMEM((TOKENS + COLS, CH), F32),
            pltpu.VMEM((TOKENS, CH), BF),
            pltpu.SemaphoreType.DMA((4,)),
        ],
        compiler_params=PARAMS,
        name="finish",
    )(tri.reshape(CH * BACK, CH), gate, gains, biases, weights)
    return update.reshape(ROWS, COLS, CH)


def solution(mesh):
    fine = Mesh(mesh.devices.reshape(4, 2, 8, 2, 2), ("y", "xl", "z", "xh", "core"))
    split = P(("y", "xl"), ("z", "xh", "core"))
    return jax.shard_map(
        body,
        mesh=fine,
        in_specs=(split, split, P(), P(), P(), P(), P(), P(), P()),
        out_specs=split,
        check_vma=False,
    )
```

```python
import jax
import jax.numpy as jnp
from jax import lax
from jax.experimental import pallas as pl
from jax.experimental.pallas import tpu as pltpu
from jax.sharding import Mesh
from jax.sharding import PartitionSpec as P

OUTWARD = ("y", "xl", "z", "xh")
HOMEWARD = ("xl", "y", "z", "xh")
LIMIT = 48 * 1024 * 1024
ROWS = 96
COLS = 24
CH = 128
SENT = 36
BACK = 18
TOKENS = ROWS * COLS
ORDER = ((0, 56, 16), (16, 24, 24), (40, 72, 24), (64, 0, 24), (88, 48, 8), (96, 0, 24), (120, 48, 8))
BF = jnp.bfloat16
F32 = jnp.float32


def dot(a, b, ca, cb):
    return lax.dot_general(a, b, (((ca,), (cb,)), ((), ())), preferred_element_type=F32)


def sigmoid(v):
    return 0.5 * jnp.tanh(0.5 * v) + 0.5


def project_kernel(
    pair, mask, gain, bias, weight, sent, pair_v, mask_v, gain_v, bias_v, weight_v, rows, out, sems
):
    parts = 1
    step = TOKENS // parts
    here = [pl.ds(part * step, step) for part in range(parts)]
    copies = [
        pltpu.make_async_copy(a, b, sems.at[n])
        for n, (a, b) in enumerate(
            [(mask, mask_v), (weight, weight_v), (gain, gain_v), (bias, bias_v)]
            + [(pair.at[h, :], pair_v.at[h, :]) for h in here]
        )
    ]
    for copy in copies:
        copy.start()
    lane = lax.broadcasted_iota(jnp.int32, (ROWS, CH), 1)
    token = lax.broadcasted_iota(jnp.int32, (ROWS, CH), 0)
    source = lane
    for start, first, count in ORDER:
        source = jnp.where((lane >= start) & (lane < start + count), lane - start + first, source)
    spread = (source == token).astype(F32).astype(BF)
    copies[0].wait()
    copies[1].wait()
    half_live = 0.5 * dot(mask_v[...].astype(F32).astype(BF), spread, 1, 0)
    turned = weight_v[...].astype(F32).T
    turned = jnp.concatenate(
        [turned[n * CH : (n + 1) * CH] * (1.0 if n % 2 else 0.5) for n in range(4)], axis=0
    ).astype(BF)
    at_lane = lax.broadcasted_iota(jnp.int32, (CH, CH), 1)

    copies[2].wait()
    copies[3].wait()
    for part in range(parts):
        copies[4 + part].wait()
        for at in range(part * step, (part + 1) * step, 192):
            x = pair_v[pl.ds(at, 192), :].astype(F32)
            mean = jnp.mean(x, axis=-1, keepdims=True)
            centred = x - mean
            var = jnp.mean(centred * centred, axis=-1, keepdims=True)
            x = centred * lax.rsqrt(var + 1e-05) * gain_v[...] + bias_v[...]
            rows[pl.ds(at, 192), :] = x

    def column(k):
        x = rows[pl.ds(k, ROWS, stride=COLS), :]
        x = jnp.concatenate([x[first : first + count] for _, first, count in ORDER], axis=0)
        x = x.astype(BF)
        proj = dot(turned, x, 1, 1)
        m = half_live[k : k + 1, :]
        left = (m * jnp.tanh(proj[:CH]) + m) * proj[CH : 2 * CH]
        right = (m * jnp.tanh(proj[2 * CH : 3 * CH]) + m) * proj[3 * CH :]
        out[pl.ds(k, CH, stride=SENT), :] = jnp.where(at_lane < ROWS, left, right)
        return right

    for k in range(12):
        low = column(k)
        high = column(k + 12)
        out[pl.ds(24 + k, CH, stride=SENT), :] = jnp.where(
            at_lane < 64, low, pltpu.roll(high, 64, 1)
        )
    sent[...] = out[pl.ds(0, CH * SENT), :].astype(BF)


SIZES = {"y": 4, "xl": 2, "z": 8, "xh": 2}


def rank_of(order, block, z, xh):
    rank = 0
    for axis in order:
        rank = rank * SIZES[axis] + {"y": block // 2, "xl": block % 2, "z": z, "xh": xh}[axis]
    return rank


STEP = rank_of(OUTWARD, 0, 1, 0)


def homeward_rows(values):
    blocks = sorted(range(8), key=lambda block: rank_of(HOMEWARD, block, 0, 0))
    starts = [rank_of(OUTWARD, block, 0, 0) for block in blocks]
    return jnp.concatenate([values[at : at + 16] for at in starts], axis=0)


def operands(chunks, wide, core):
    wide[pl.ds(0, CH * SENT), :] = chunks[...].astype(F32)
    shifts = jnp.where(core == 0, 32, 112), jnp.where(core == 0, 96, 48)
    lane = lax.broadcasted_iota(jnp.int32, (384, CH), 1)
    lefts, rights = [], []
    for block in range(8):
        starts = [rank_of(OUTWARD, block, 0, xh) * SENT for xh in range(2)]

        def gather(ks):
            return jnp.concatenate(
                [wide[pl.ds(at + k, 8, stride=SENT * STEP), :] for k in ks for at in starts],
                axis=0,
            )

        left = gather(range(24))
        mid = gather(range(24, SENT))
        right = jnp.concatenate([mid, pltpu.roll(mid, 64, 1)], axis=0)
        right = jnp.where(lane < 64, right, left)
        rights.append(pltpu.roll(right, shifts[block % 2], 1))
        lefts.append(left.astype(BF))
    pairs = [
        jnp.where(lane < 64, rights[2 * n], rights[2 * n + 1]).astype(BF)
        for n in range(4)
    ]
    return jnp.concatenate(lefts, axis=1), pairs


def product_own_kernel(
    core, chunks, pair, in_gain, in_bias, gate_weight, gain, bias, weight, total, gate, gains, biases, weights, wide
):
    left, rights = operands(chunks, wide, core[0])
    for n in range(4):
        total[pl.ds(n * CH, CH), :] = dot(rights[n].T, left, 1, 0)
    for at in range(0, TOKENS, 256):
        here = pl.ds(at, 256)
        x = pair[here, :].astype(F32)
        centred = x - jnp.mean(x, axis=-1, keepdims=True)
        var = jnp.mean(centred * centred, axis=-1, keepdims=True)
        x = centred * lax.rsqrt(var + 1e-05) * in_gain[...] + in_bias[...]
        gate[here, :] = sigmoid(dot(x.astype(BF), gate_weight[...], 1, 0))
    gains[...] = homeward_rows(jnp.broadcast_to(gain[...], (CH, CH)).T)
    biases[...] = homeward_rows(jnp.broadcast_to(bias[...], (CH, CH)).T)
    weights[...] = homeward_rows(weight[...])


def product_other_kernel(core, chunks, total, sent, wide, packed):
    left, rights = operands(chunks, wide, core[0])
    lane = lax.broadcasted_iota(jnp.int32, (BACK, CH), 1)
    for n in range(4):
        tri = total[pl.ds(n * CH, CH), :] + dot(rights[n].T, left, 1, 0)
        for part, at in enumerate((0, 24, 64, 88)):
            for block in range(8):
                here = tri[at : at + 24, block * CH : (block + 1) * CH]
                tail = here[BACK:]
                tail = jnp.concatenate([pltpu.roll(tail, 96 - 32 * g, 1) for g in range(3)], axis=0)
                chip = n * 4 + part
                rank = rank_of(HOMEWARD, block, chip // 2, chip % 2)
                packed[pl.ds(rank * BACK, BACK), :] = jnp.where(
                    lane < ROWS, here[:BACK], tail
                )
    sent[...] = packed[pl.ds(0, CH * BACK), :].astype(BF)


def finish_kernel(tri, gate, gain, bias, weight, update, cols, out, done, sems):
    cols[pl.ds(0, CH * BACK), :] = tri[...].astype(F32)
    for row in range(BACK):
        v = cols[pl.ds(row, CH, stride=BACK), :]
        mean = jnp.mean(v, axis=0, keepdims=True)
        centred = v - mean
        var = jnp.mean(centred * centred, axis=0, keepdims=True)
        v = (centred * lax.rsqrt(var + 1e-05) * gain[...] + bias[...]).astype(BF)
        mixed = dot(v, weight[...], 0, 0)
        for start, first, count in ORDER[:5]:
            out[pl.ds(first * COLS + row, count, stride=COLS), :] = mixed[start : start + count]
        group = row // 6
        for start, first, count in ORDER[:5]:
            low, high = max(start, 32 * group), min(start + count, 32 * group + 32)
            if low < high:
                out[pl.ds((first + low - start) * COLS + BACK + row % 6, high - low, stride=COLS), :] = (
                    mixed[ROWS + low - 32 * group : ROWS + high - 32 * group]
                )
    parts = 4
    step = TOKENS // parts
    copies = []
    for part in range(parts):
        here = pl.ds(part * step, step)
        done[here, :] = (gate[here, :] * out[here, :]).astype(BF)
        copies.append(pltpu.make_async_copy(done.at[here, :], update.at[here, :], sems.at[part]))
        copies[-1].start()
    for copy in copies:
        copy.wait()


VMEM = pl.BlockSpec(memory_space=pltpu.VMEM)
SMEM = pl.BlockSpec(memory_space=pltpu.SMEM)
HBM = pl.BlockSpec(memory_space=pltpu.HBM)
PARAMS = pltpu.CompilerParams(vmem_limit_bytes=LIMIT)


def in_hbm(x):
    return pltpu.with_memory_space_constraint(x, pltpu.HBM)


def body(
    pair, pair_mask, in_gain, in_bias, input_proj, gate_weight, out_gain, out_bias, out_weight
):
    sent = pl.pallas_call(
        project_kernel,
        out_shape=pltpu.VMEM((CH * SENT, CH), BF),
        in_specs=[HBM] * 5,
        out_specs=VMEM,
        scratch_shapes=[
            pltpu.VMEM((TOKENS, CH), BF),
            pltpu.VMEM((COLS, ROWS), jnp.int32),
            pltpu.VMEM((1, CH), F32),
            pltpu.VMEM((1, CH), F32),
            pltpu.VMEM((CH, 4 * CH), BF),
            pltpu.VMEM((TOKENS + COLS, CH), F32),
            pltpu.VMEM((CH * SENT + SENT, CH), F32),
            pltpu.SemaphoreType.DMA((8,)),
        ],
        compiler_params=PARAMS,
        name="project",
    )(
        in_hbm(pair.reshape(TOKENS, CH)),
        in_hbm(pair_mask.T),
        in_hbm(in_gain.reshape(1, CH)),
        in_hbm(in_bias.reshape(1, CH)),
        in_hbm(input_proj),
    )
    own = lax.all_to_all(sent.reshape(CH, 9, 4, CH), OUTWARD, 0, 0, tiled=True)
    other = lax.ppermute(own, "core", [(0, 1), (1, 0)])
    core = lax.axis_index("core").astype(jnp.int32).reshape(1)
    total, gate, gains, biases, weights = pl.pallas_call(
        product_own_kernel,
        out_shape=(
            pltpu.VMEM((4 * CH, 8 * CH), F32),
            pltpu.VMEM((TOKENS, CH), F32),
            pltpu.VMEM((CH, CH), F32),
            pltpu.VMEM((CH, CH), F32),
            pltpu.VMEM((CH, CH), BF),
        ),
        in_specs=[SMEM] + [VMEM] * 8,
        out_specs=[VMEM] * 5,
        scratch_shapes=[pltpu.VMEM((CH * SENT + STEP * SENT, CH), F32)],
        compiler_params=PARAMS,
        cost_estimate=pl.CostEstimate(flops=4 * 10**8, bytes_accessed=4 * 10**6, transcendentals=0),
        name="product_own",
    )(
        core,
        own.reshape(CH * SENT, CH),
        pair.reshape(TOKENS, CH),
        in_gain.reshape(1, CH),
        in_bias.reshape(1, CH),
        gate_weight,
        out_gain.reshape(1, CH),
        out_bias.reshape(1, CH),
        out_weight,
    )
    tri = pl.pallas_call(
        product_other_kernel,
        out_shape=pltpu.VMEM((CH * BACK, CH), BF),
        in_specs=[SMEM, VMEM, VMEM],
        out_specs=VMEM,
        scratch_shapes=[
            pltpu.VMEM((CH * SENT + STEP * SENT, CH), F32),
            pltpu.VMEM((CH * BACK + 8, CH), F32),
        ],
        compiler_params=PARAMS,
        name="product_other",
    )(core, other.reshape(CH * SENT, CH), total)
    tri = lax.all_to_all(tri.reshape(CH, 9, 2, CH), HOMEWARD, 0, 0, tiled=True)
    update = pl.pallas_call(
        finish_kernel,
        out_shape=jax.ShapeDtypeStruct((TOKENS, CH), BF),
        in_specs=[VMEM] * 5,
        out_specs=HBM,
        scratch_shapes=[
            pltpu.VMEM((CH * BACK + BACK, CH), F32),
            pltpu.VMEM((TOKENS + COLS, CH), F32),
            pltpu.VMEM((TOKENS, CH), BF),
            pltpu.SemaphoreType.DMA((4,)),
        ],
        compiler_params=PARAMS,
        name="finish",
    )(tri.reshape(CH * BACK, CH), gate, gains, biases, weights)
    return update.reshape(ROWS, COLS, CH)


def solution(mesh):
    fine = Mesh(mesh.devices.reshape(4, 2, 8, 2, 2), ("y", "xl", "z", "xh", "core"))
    split = P(("y", "xl"), ("z", "xh", "core"))
    return jax.shard_map(
        body,
        mesh=fine,
        in_specs=(split, split, P(), P(), P(), P(), P(), P(), P()),
        out_specs=split,
        check_vma=False,
    )
```

```python
import jax
import jax.numpy as jnp
from jax import lax
from jax.experimental import pallas as pl
from jax.experimental.pallas import tpu as pltpu
from jax.sharding import Mesh
from jax.sharding import PartitionSpec as P

OUTWARD = ("y", "xl", "z", "xh")
HOMEWARD = ("xl", "y", "z", "xh")
LIMIT = 48 * 1024 * 1024
ROWS = 96
COLS = 24
CH = 128
SENT = 36
BACK = 18
TOKENS = ROWS * COLS
ORDER = ((0, 56, 16), (16, 24, 24), (40, 72, 24), (64, 0, 24), (88, 48, 8), (96, 0, 24), (120, 48, 8))
BF = jnp.bfloat16
F32 = jnp.float32


def dot(a, b, ca, cb):
    return lax.dot_general(a, b, (((ca,), (cb,)), ((), ())), preferred_element_type=F32)


def sigmoid(v):
    return 0.5 * jnp.tanh(0.5 * v) + 0.5


def project_kernel(
    pair, mask, gain, bias, weight, sent, normed, pair_v, mask_v, gain_v, bias_v, weight_v, rows, out, sems
):
    parts = 1
    step = TOKENS // parts
    here = [pl.ds(part * step, step) for part in range(parts)]
    copies = [
        pltpu.make_async_copy(a, b, sems.at[n])
        for n, (a, b) in enumerate(
            [(mask, mask_v), (weight, weight_v), (gain, gain_v), (bias, bias_v)]
            + [(pair.at[h, :], pair_v.at[h, :]) for h in here]
        )
    ]
    for copy in copies:
        copy.start()
    lane = lax.broadcasted_iota(jnp.int32, (ROWS, CH), 1)
    token = lax.broadcasted_iota(jnp.int32, (ROWS, CH), 0)
    source = lane
    for start, first, count in ORDER:
        source = jnp.where((lane >= start) & (lane < start + count), lane - start + first, source)
    spread = (source == token).astype(F32).astype(BF)
    copies[0].wait()
    copies[1].wait()
    half_live = 0.5 * dot(mask_v[...].astype(F32).astype(BF), spread, 1, 0)
    turned = weight_v[...].astype(F32).T
    turned = jnp.concatenate(
        [turned[n * CH : (n + 1) * CH] * (1.0 if n % 2 else 0.5) for n in range(4)], axis=0
    ).astype(BF)
    at_lane = lax.broadcasted_iota(jnp.int32, (CH, CH), 1)

    copies[2].wait()
    copies[3].wait()
    for part in range(parts):
        copies[4 + part].wait()
        for at in range(part * step, (part + 1) * step, 192):
            x = pair_v[pl.ds(at, 192), :].astype(F32)
            mean = jnp.mean(x, axis=-1, keepdims=True)
            centred = x - mean
            var = jnp.mean(centred * centred, axis=-1, keepdims=True)
            x = centred * lax.rsqrt(var + 1e-05) * gain_v[...] + bias_v[...]
            normed[pl.ds(at, 192), :] = x.astype(BF)
            rows[pl.ds(at, 192), :] = x

    def column(k):
        x = rows[pl.ds(k, ROWS, stride=COLS), :]
        x = jnp.concatenate([x[first : first + count] for _, first, count in ORDER], axis=0)
        x = x.astype(BF)
        proj = dot(turned, x, 1, 1)
        m = half_live[k : k + 1, :]
        left = (m * jnp.tanh(proj[:CH]) + m) * proj[CH : 2 * CH]
        right = (m * jnp.tanh(proj[2 * CH : 3 * CH]) + m) * proj[3 * CH :]
        out[pl.ds(k, CH, stride=SENT), :] = jnp.where(at_lane < ROWS, left, right)
        return right

    for k in range(12):
        low = column(k)
        high = column(k + 12)
        out[pl.ds(24 + k, CH, stride=SENT), :] = jnp.where(
            at_lane < 64, low, pltpu.roll(high, 64, 1)
        )
    sent[...] = out[pl.ds(0, CH * SENT), :].astype(BF)


SIZES = {"y": 4, "xl": 2, "z": 8, "xh": 2}


def rank_of(order, block, z, xh):
    rank = 0
    for axis in order:
        rank = rank * SIZES[axis] + {"y": block // 2, "xl": block % 2, "z": z, "xh": xh}[axis]
    return rank


STEP = rank_of(OUTWARD, 0, 1, 0)


def homeward_rows(values):
    blocks = sorted(range(8), key=lambda block: rank_of(HOMEWARD, block, 0, 0))
    starts = [rank_of(OUTWARD, block, 0, 0) for block in blocks]
    return jnp.concatenate([values[at : at + 16] for at in starts], axis=0)


def operands(chunks, wide, core):
    wide[pl.ds(0, CH * SENT), :] = chunks[...].astype(F32)
    shifts = jnp.where(core == 0, 32, 112), jnp.where(core == 0, 96, 48)
    lane = lax.broadcasted_iota(jnp.int32, (384, CH), 1)
    lefts, rights = [], []
    for block in range(8):
        starts = [rank_of(OUTWARD, block, 0, xh) * SENT for xh in range(2)]

        def gather(ks):
            return jnp.concatenate(
                [wide[pl.ds(at + k, 8, stride=SENT * STEP), :] for k in ks for at in starts],
                axis=0,
            )

        left = gather(range(24))
        mid = gather(range(24, SENT))
        right = jnp.concatenate([mid, pltpu.roll(mid, 64, 1)], axis=0)
        right = jnp.where(lane < 64, right, left)
        rights.append(pltpu.roll(right, shifts[block % 2], 1))
        lefts.append(left.astype(BF))
    pairs = [
        jnp.where(lane < 64, rights[2 * n], rights[2 * n + 1]).astype(BF)
        for n in range(4)
    ]
    return jnp.concatenate(lefts, axis=1), pairs


def product_own_kernel(
    core, chunks, normed, gate_weight, gain, bias, weight, total, gate, gains, biases, weights, wide
):
    left, rights = operands(chunks, wide, core[0])
    for n in range(4):
        total[pl.ds(n * CH, CH), :] = dot(rights[n].T, left, 1, 0)
    for at in range(0, TOKENS, 256):
        here = pl.ds(at, 256)
        gate[here, :] = sigmoid(dot(normed[here, :], gate_weight[...], 1, 0))
    gains[...] = homeward_rows(jnp.broadcast_to(gain[...], (CH, CH)).T)
    biases[...] = homeward_rows(jnp.broadcast_to(bias[...], (CH, CH)).T)
    weights[...] = homeward_rows(weight[...])


def product_other_kernel(core, chunks, total, sent, wide, packed):
    left, rights = operands(chunks, wide, core[0])
    lane = lax.broadcasted_iota(jnp.int32, (BACK, CH), 1)
    for n in range(4):
        tri = total[pl.ds(n * CH, CH), :] + dot(rights[n].T, left, 1, 0)
        for part, at in enumerate((0, 24, 64, 88)):
            for block in range(8):
                here = tri[at : at + 24, block * CH : (block + 1) * CH]
                tail = here[BACK:]
                tail = jnp.concatenate([pltpu.roll(tail, 96 - 32 * g, 1) for g in range(3)], axis=0)
                chip = n * 4 + part
                rank = rank_of(HOMEWARD, block, chip // 2, chip % 2)
                packed[pl.ds(rank * BACK, BACK), :] = jnp.where(
                    lane < ROWS, here[:BACK], tail
                )
    sent[...] = packed[pl.ds(0, CH * BACK), :].astype(BF)


def finish_kernel(tri, gate, gain, bias, weight, update, cols, out, done, sems):
    cols[pl.ds(0, CH * BACK), :] = tri[...].astype(F32)
    for row in range(BACK):
        v = cols[pl.ds(row, CH, stride=BACK), :]
        mean = jnp.mean(v, axis=0, keepdims=True)
        centred = v - mean
        var = jnp.mean(centred * centred, axis=0, keepdims=True)
        v = (centred * lax.rsqrt(var + 1e-05) * gain[...] + bias[...]).astype(BF)
        mixed = dot(v, weight[...], 0, 0)
        for start, first, count in ORDER[:5]:
            out[pl.ds(first * COLS + row, count, stride=COLS), :] = mixed[start : start + count]
        group = row // 6
        for start, first, count in ORDER[:5]:
            low, high = max(start, 32 * group), min(start + count, 32 * group + 32)
            if low < high:
                out[pl.ds((first + low - start) * COLS + BACK + row % 6, high - low, stride=COLS), :] = (
                    mixed[ROWS + low - 32 * group : ROWS + high - 32 * group]
                )
    parts = 2
    step = TOKENS // parts
    copies = []
    for part in range(parts):
        here = pl.ds(part * step, step)
        done[here, :] = (gate[here, :] * out[here, :]).astype(BF)
        copies.append(pltpu.make_async_copy(done.at[here, :], update.at[here, :], sems.at[part]))
        copies[-1].start()
    for copy in copies:
        copy.wait()


VMEM = pl.BlockSpec(memory_space=pltpu.VMEM)
SMEM = pl.BlockSpec(memory_space=pltpu.SMEM)
HBM = pl.BlockSpec(memory_space=pltpu.HBM)
PARAMS = pltpu.CompilerParams(vmem_limit_bytes=LIMIT)


def in_hbm(x):
    return pltpu.with_memory_space_constraint(x, pltpu.HBM)


def body(
    pair, pair_mask, in_gain, in_bias, input_proj, gate_weight, out_gain, out_bias, out_weight
):
    sent, normed = pl.pallas_call(
        project_kernel,
        out_shape=(
            pltpu.VMEM((CH * SENT, CH), BF),
            pltpu.VMEM((TOKENS, CH), BF),
        ),
        in_specs=[HBM] * 5,
        out_specs=(VMEM, VMEM),
        scratch_shapes=[
            pltpu.VMEM((TOKENS, CH), BF),
            pltpu.VMEM((COLS, ROWS), jnp.int32),
            pltpu.VMEM((1, CH), F32),
            pltpu.VMEM((1, CH), F32),
            pltpu.VMEM((CH, 4 * CH), BF),
            pltpu.VMEM((TOKENS + COLS, CH), F32),
            pltpu.VMEM((CH * SENT + SENT, CH), F32),
            pltpu.SemaphoreType.DMA((8,)),
        ],
        compiler_params=PARAMS,
        name="project",
    )(
        in_hbm(pair.reshape(TOKENS, CH)),
        in_hbm(pair_mask.T),
        in_hbm(in_gain.reshape(1, CH)),
        in_hbm(in_bias.reshape(1, CH)),
        in_hbm(input_proj),
    )
    own = lax.all_to_all(sent.reshape(CH, 9, 4, CH), OUTWARD, 0, 0, tiled=True)
    other = lax.ppermute(own, "core", [(0, 1), (1, 0)])
    core = lax.axis_index("core").astype(jnp.int32).reshape(1)
    total, gate, gains, biases, weights = pl.pallas_call(
        product_own_kernel,
        out_shape=(
            pltpu.VMEM((4 * CH, 8 * CH), F32),
            pltpu.VMEM((TOKENS, CH), F32),
            pltpu.VMEM((CH, CH), F32),
            pltpu.VMEM((CH, CH), F32),
            pltpu.VMEM((CH, CH), BF),
        ),
        in_specs=[SMEM] + [VMEM] * 6,
        out_specs=[VMEM] * 5,
        scratch_shapes=[pltpu.VMEM((CH * SENT + STEP * SENT, CH), F32)],
        compiler_params=PARAMS,
        cost_estimate=pl.CostEstimate(flops=4 * 10**8, bytes_accessed=4 * 10**6, transcendentals=0),
        name="product_own",
    )(
        core,
        own.reshape(CH * SENT, CH),
        normed,
        gate_weight,
        out_gain.reshape(1, CH),
        out_bias.reshape(1, CH),
        out_weight,
    )
    tri = pl.pallas_call(
        product_other_kernel,
        out_shape=pltpu.VMEM((CH * BACK, CH), BF),
        in_specs=[SMEM, VMEM, VMEM],
        out_specs=VMEM,
        scratch_shapes=[
            pltpu.VMEM((CH * SENT + STEP * SENT, CH), F32),
            pltpu.VMEM((CH * BACK + 8, CH), F32),
        ],
        compiler_params=PARAMS,
        name="product_other",
    )(core, other.reshape(CH * SENT, CH), total)
    tri = lax.all_to_all(tri.reshape(CH, 9, 2, CH), HOMEWARD, 0, 0, tiled=True)
    update = pl.pallas_call(
        finish_kernel,
        out_shape=jax.ShapeDtypeStruct((TOKENS, CH), BF),
        in_specs=[VMEM] * 5,
        out_specs=HBM,
        scratch_shapes=[
            pltpu.VMEM((CH * BACK + BACK, CH), F32),
            pltpu.VMEM((TOKENS + COLS, CH), F32),
            pltpu.VMEM((TOKENS, CH), BF),
            pltpu.SemaphoreType.DMA((2,)),
        ],
        compiler_params=PARAMS,
        name="finish",
    )(tri.reshape(CH * BACK, CH), gate, gains, biases, weights)
    return update.reshape(ROWS, COLS, CH)


def solution(mesh):
    fine = Mesh(mesh.devices.reshape(4, 2, 8, 2, 2), ("y", "xl", "z", "xh", "core"))
    split = P(("y", "xl"), ("z", "xh", "core"))
    return jax.shard_map(
        body,
        mesh=fine,
        in_specs=(split, split, P(), P(), P(), P(), P(), P(), P()),
        out_specs=split,
        check_vma=False,
    )
```
